32 devices in a mesh: dp: 8 (over y, x, core), mp: 4 (over z).
Axes of the slice: x: 2, y: 2, z: 4, core: 2. Of those that a mesh axis runs over, the one named last changes fastest.
Arguments:
- inputs: bfloat16 [16, 16, 4096], P('dp')
- denoiser: int32 [16], P('dp'), may hold values from 0 to 2
- span_mask: int32 [16, 16], P('dp'), may hold values 0 or 1
- lengths: int32 [16], P('dp'), may hold values from 4 to 16
- move_plan: int32 [16], P('dp'), may hold values from -1 to 1, as said below
- mode_table: bfloat16 [3, 4096], replicated, may hold values from -3 to 3
- sentinel: bfloat16 [4096], replicated, may hold values from -6 to 6
- w_query: bfloat16 [4096, 1024], P(None, 'mp')
- w_key: bfloat16 [4096, 1024], P(None, 'mp')
- w_value: bfloat16 [4096, 1024], P(None, 'mp'), may hold values from -0.09375 to 0.09375
- cotangent: bfloat16 [32, 16, 1024], P('dp', None, 'mp'), may hold values from -6 to 6
Outputs:
- context: bfloat16 [32, 16, 1024], P('dp', None, 'mp')
- input_grad: bfloat16 [16, 16, 4096], P('dp', 'mp')
The draws below stay inside these ranges and needn't reach their ends.
Inputs may be any that keep to these rules, and one draw needn't show every extreme that they name: `move_plan`: every row stays (0) or moves to the next (1) or previous (-1) data group along dp, cyclically. A data group sends at most one row to each of its two neighbours, and in every draw some data group receives a row from both neighbours.
All inputs are finite; a program needn't handle non-finite values. No bound on the sum of `span_mask` on one device may be relied on, other than what follows from the above.
Results may differ from the reference program's by a relative error of at most 0.02.
The reference program's roundings to bfloat16 on the way count: a program that leaves them out, or rounds other values in their place, can miss the bound.
Values may be sent and summed in bfloat16 or wider, within the bound.
A program may use at most 64 MiB of HBM per device.

```python
import math
import jax
import jax.numpy as jnp
from jax import lax

D = 4096
HD = 256
HEADS = 4
LENGTH = 16
ROWS_DEV = 2
HOLD = 4
ROWS = 16
SLOTS = 32
MODES = 3
N_DP = 8


def draw_inputs(key, part):
    key = jax.random.fold_in(key, 3)
    keys = jax.random.split(key, 1)
    values = jax.random.normal(keys[0], (ROWS, LENGTH, D), jnp.float32)
    return values.astype(jnp.bfloat16)


def drawn_weight(key):
    values = jax.random.normal(key, (D, HEADS * HD), jnp.float32) / math.sqrt(D)
    return values.astype(jnp.bfloat16)


def draw_w_query(key, part):
    key = jax.random.fold_in(key, 5)
    return drawn_weight(key)


def draw_w_key(key, part):
    key = jax.random.fold_in(key, 7)
    return drawn_weight(key)


def draw_lengths(key, part):
    key = jax.random.fold_in(key, 11)
    keys = jax.random.split(key, 3)
    values = jax.random.randint(keys[0], (ROWS,), LENGTH // 4, LENGTH + 1)
    first = jax.random.randint(keys[1], (), 0, ROWS)
    second = (first + 1 + jax.random.randint(keys[2], (), 0, ROWS - 1)) % ROWS
    values = values.at[first].set(LENGTH)
    values = values.at[second].set(LENGTH // 4)
    return values.astype(jnp.int32)


def draw_move_plan(key, part):
    key = jax.random.fold_in(key, 13)
    keys = jax.random.split(key, 4)
    group_count = ROWS // ROWS_DEV
    scores = jax.random.randint(keys[0], (group_count, ROWS_DEV), 0, 2 ** 20) * ROWS_DEV
    scores = scores + jnp.arange(ROWS_DEV, dtype=jnp.int32)[None, :]
    order = jnp.argsort(scores, axis=1, stable=True).astype(jnp.int32)
    send_right = jax.random.randint(keys[1], (group_count,), 0, 2)
    send_left = jax.random.randint(keys[2], (group_count,), 0, 2)
    chosen = jax.random.randint(keys[3], (), 0, group_count)
    partner = (chosen + 2) % group_count
    groups = jnp.arange(group_count, dtype=jnp.int32)
    send_right = jnp.where(groups == chosen, 1, jnp.where(groups == partner, 0, send_right))
    send_left = jnp.where(groups == chosen, 0, jnp.where(groups == partner, 1, send_left))
    local = jnp.arange(ROWS_DEV, dtype=jnp.int32)[None, :]
    right_row = (local == order[:, 0:1]) & (send_right[:, None] == 1)
    left_row = (local == order[:, 1:2]) & (send_left[:, None] == 1)
    plan = jnp.where(right_row, 1, jnp.where(left_row, -1, 0))
    return plan.reshape(ROWS).astype(jnp.int32)


def with_ends(drawn, own_key, least, top_value):
    spot = [jax.random.randint(jax.random.fold_in(own_key, axis), (), 0, length) for axis, length in enumerate(drawn.shape)]
    main_axis = drawn.shape.index(max(drawn.shape))
    beside = spot[:main_axis] + [(spot[main_axis] + 1) % drawn.shape[main_axis]] + spot[main_axis + 1:]
    return drawn.at[tuple(spot)].set(least).at[tuple(beside)].set(top_value)


def block_scale(stream_key, extent, pieces, low, high):
    gain = 1.0
    for axis_at, shards_of in pieces:
        heights = jax.random.uniform(jax.random.fold_in(jax.random.fold_in(stream_key, 6), axis_at), (shards_of,), jnp.float32, low / len(pieces), high / len(pieces))
        gain = gain * jnp.repeat(jnp.exp(heights), extent[axis_at] // shards_of).reshape((-1,) + (1,) * (len(extent) - 1 - axis_at))
    return gain


def gaussian(rng, extent, spread, bound, cuts=(), kind=jnp.bfloat16):
    values = jax.random.normal(rng, extent, jnp.float32) * spread
    if len(cuts) > 0:
        values = block_scale(rng, extent, cuts, -0.22, 0.18) * values
    return jnp.clip(values, min=-bound, max=bound).astype(kind)


def setup_inputs(seed: int = 0) -> dict:
    key_list = jax.random.split(jax.random.key(seed), 12)
    return {
        "inputs": draw_inputs(jax.random.fold_in(key_list[11], 71), 0),
        "denoiser": with_ends(jax.random.randint(key_list[1], (ROWS,), 0, 3), jax.random.fold_in(key_list[1], 1), 0, 2).astype(jnp.int32),
        "span_mask": with_ends((jax.random.randint(key_list[2], (ROWS, LENGTH), 0, 20) < 3).astype(jnp.int32), jax.random.fold_in(key_list[2], 1), 0, 1),
        "lengths": draw_lengths(jax.random.fold_in(key_list[11], 71), 0),
        "move_plan": draw_move_plan(jax.random.fold_in(key_list[11], 71), 0),
        "mode_table": gaussian(key_list[5], (MODES, D), 0.5, 3.0),
        "sentinel": gaussian(key_list[6], (D,), 1.0, 6.0),
        "w_query": draw_w_query(jax.random.fold_in(key_list[11], 71), 0),
        "w_key": draw_w_key(jax.random.fold_in(key_list[11], 71), 0),
        "w_value": gaussian(key_list[9], (D, HEADS * HD), D ** -0.5, 0.09375, ((1, 4),)),
        "cotangent": gaussian(key_list[10], (SLOTS, LENGTH, HEADS * HD), 1.0, 6.0, ((0, 8), (2, 4))),
    }


def rounded(values):
    return lax.optimization_barrier(values.astype(jnp.bfloat16))

def attend_slot(slot_rows, slot_len, cotangent, w_query, w_key, w_value, query_full, key_full, value_full):
    flat_rows = slot_rows.astype(jnp.float32)
    inv_rms = lax.rsqrt(lax.optimization_barrier(jnp.mean(flat_rows * flat_rows, axis=1, keepdims=True)) + 1e-06)
    normed = flat_rows * inv_rms
    normed_b = normed.astype(jnp.bfloat16)

    def project(weight):
        result = jnp.dot(normed_b, weight, preferred_element_type=jnp.float32)
        return rounded(result).astype(jnp.float32).reshape(LENGTH, HEADS, HD)
    query_rows = project(w_query)
    key_rows = project(w_key)
    value_rows = project(w_value)
    positions = jnp.arange(LENGTH, dtype=jnp.int32)
    key_ok = (positions < jnp.maximum(slot_len, 1))[None, None, :]
    query_ok = positions < slot_len
    factor = 1.0 / math.sqrt(HD)
    scores = jnp.einsum('qhd,khd->hqk', query_rows, key_rows) * factor
    scores = jnp.where(key_ok, scores, -jnp.inf)
    row_max = lax.optimization_barrier(jnp.max(scores, axis=2, keepdims=True))
    exp_scores = jnp.exp(scores - row_max)
    soft = exp_scores / lax.optimization_barrier(jnp.sum(exp_scores, axis=2, keepdims=True))
    soft_b = rounded(soft).astype(jnp.float32)
    context = jnp.einsum('hqk,khd->qhd', soft_b, value_rows)
    context = context * query_ok[:, None, None].astype(jnp.float32)
    context = context.astype(jnp.bfloat16).reshape(LENGTH, HEADS * HD)
    grad_out = cotangent.reshape(LENGTH, HEADS, HD).astype(jnp.float32)
    grad_out = jnp.where(query_ok[:, None, None], grad_out, jnp.zeros_like(grad_out))
    grad_value = rounded(jnp.einsum('hqk,qhd->khd', soft_b, grad_out)).astype(jnp.float32)
    grad_soft = jnp.einsum('qhd,khd->hqk', grad_out, value_rows)
    row_inner = lax.optimization_barrier(jnp.sum(soft * grad_soft, axis=2, keepdims=True))
    grad_scores = rounded(soft * (grad_soft - row_inner) * factor).astype(jnp.float32)
    grad_query = rounded(jnp.einsum('hqk,khd->qhd', grad_scores, key_rows)).astype(jnp.float32)
    grad_key = rounded(jnp.einsum('hqk,qhd->khd', grad_scores, query_rows)).astype(jnp.float32)
    head_grad = jnp.einsum('qhd,ehd->hqe', grad_query, query_full)
    head_grad = head_grad + jnp.einsum('qhd,ehd->hqe', grad_key, key_full)
    head_grad = head_grad + jnp.einsum('qhd,ehd->hqe', grad_value, value_full)
    inner_norm = lax.optimization_barrier(jnp.mean(head_grad * normed[None, :, :], axis=2, keepdims=True))
    head_part = rounded((head_grad - normed[None, :, :] * inner_norm) * inv_rms[None, :, :])
    slot_grad = lax.optimization_barrier(jnp.sum(head_part.astype(jnp.float32), axis=0)).astype(jnp.bfloat16)
    return (context, slot_grad)

def reference(inputs, denoiser, span_mask, lengths, move_plan, mode_table, sentinel, w_query, w_key, w_value, cotangent):
    mode_rows = mode_table.astype(jnp.float32)[denoiser]
    span_flag = (span_mask == 1)[:, :, None]
    shaped = jnp.where(span_flag, sentinel.astype(jnp.float32)[None, None, :], inputs.astype(jnp.float32) + mode_rows[:, None, :]).astype(jnp.bfloat16)
    groups = jnp.arange(N_DP, dtype=jnp.int32)[:, None]
    local = jnp.arange(ROWS_DEV, dtype=jnp.int32)[None, :]
    moves = move_plan.reshape(N_DP, ROWS_DEV)
    target = jnp.where(moves == 1, (groups + 1) % N_DP * HOLD + ROWS_DEV, jnp.where(moves == -1, (groups + N_DP - 1) % N_DP * HOLD + ROWS_DEV + 1, groups * HOLD + local)).reshape(ROWS).astype(jnp.int32)
    sources = jnp.zeros((SLOTS,), jnp.int32).at[target].set(jnp.arange(ROWS, dtype=jnp.int32))
    filled = jnp.zeros((SLOTS,), jnp.bool_).at[target].set(True)
    slot_len = jnp.where(filled, lengths[sources], 0).astype(jnp.int32)
    query_full = w_query.astype(jnp.float32).reshape(D, HEADS, HD)
    key_full = w_key.astype(jnp.float32).reshape(D, HEADS, HD)
    value_full = w_value.astype(jnp.float32).reshape(D, HEADS, HD)

    def one_slot(slot):
        return attend_slot(shaped[sources[slot]], slot_len[slot], cotangent[slot], w_query, w_key, w_value, query_full, key_full, value_full)
    context, slot_grad = lax.map(one_slot, jnp.arange(SLOTS, dtype=jnp.int32))
    input_grad = slot_grad[target]
    input_grad = jnp.where(span_flag, jnp.zeros_like(input_grad), input_grad)
    return (context, input_grad)
```

```python
import functools
import math

import jax
import jax.numpy as jnp
from jax import lax
from jax.experimental import pallas as pl
from jax.experimental.pallas import tpu as pltpu
from jax.sharding import PartitionSpec as P

MESH = pl.DeviceIdType.MESH
F32 = jnp.float32
BF16 = jnp.bfloat16
NT = (((1,), (1,)), ((), ()))
TN = (((0,), (0,)), ((), ()))
NN = (((1,), (0,)), ((), ()))

FORWARD_CHUNKS = 4
BACK_CHUNKS = 4
NORM_CHUNKS = 8


def matmul(a, b, dims=NN):
    return lax.dot_general(a, b, dims, preferred_element_type=F32)


def kernel(
    dp_count,
    mp_count,
    denoiser_ref,
    lengths_ref,
    move_ref,
    span_ref,
    table_ref,
    sentinel_ref,
    inputs_hbm,
    cot_hbm,
    wq_hbm,
    wk_hbm,
    wv_hbm,
    context_ref,
    grad_ref,
    inputs_ref,
    cot_ref,
    weights,
    normed_ref,
    normed_b_ref,
    cot_recv,
    ctx_send,
    part_send,
    part_recv,
    in_sem,
    w_sem,
    cot_send_sem,
    cot_recv_sem,
    ctx_send_sem,
    ctx_recv_sem,
    part_send_sem,
    part_recv_sem,
):
    rows, length, width = inputs_ref.shape
    head = weights.shape[2]
    seg = length // mp_count
    total = rows * length
    seg_total = rows * seg
    mode_count = table_ref.shape[0]
    my_dp = lax.axis_index("dp")
    my_mp = lax.axis_index("mp")
    right = lax.rem(my_dp + 1, dp_count)
    left = lax.rem(my_dp + dp_count - 1, dp_count)

    barrier = pltpu.get_barrier_semaphore()
    for neighbour in (left, right):
        pl.semaphore_signal(barrier, inc=1, device_id={"dp": neighbour}, device_id_type=MESH)
    for step in range(1, mp_count):
        pl.semaphore_signal(
            barrier,
            inc=1,
            device_id={"mp": lax.rem(my_mp + step, mp_count)},
            device_id_type=MESH,
        )

    load_inputs = pltpu.make_async_copy(inputs_hbm, inputs_ref, in_sem.at[0])
    load_inputs.start()
    load_cot = pltpu.make_async_copy(cot_hbm.at[pl.ds(0, rows)], cot_ref, in_sem.at[1])
    load_cot.start()
    depth = width // FORWARD_CHUNKS
    loads = []
    for which, source in enumerate((wq_hbm, wk_hbm, wv_hbm)):
        for chunk in range(FORWARD_CHUNKS):
            piece = pl.ds(chunk * depth, depth)
            load = pltpu.make_async_copy(
                source.at[piece], weights.at[which, piece], w_sem.at[which, chunk]
            )
            load.start()
            loads.append(load)

    def split(index):
        row = lax.rem(lax.div(index, seg), rows)
        place = lax.div(index, seg_total) * seg + lax.rem(index, seg)
        return row, place

    def per_row(row, ref):
        value = jnp.zeros_like(row)
        for r in range(rows):
            value = jnp.where(row == r, ref[r], value)
        return value

    col_row, col_place = split(lax.broadcasted_iota(jnp.int32, (total, 1), 0))
    lane_row, lane_place = split(lax.broadcasted_iota(jnp.int32, (1, total), 1))
    natural_lane = lax.broadcasted_iota(jnp.int32, (total, total), 1)
    permute = (natural_lane == col_row * length + col_place).astype(F32).astype(BF16)
    col_len = per_row(col_row, lengths_ref)
    key_ok = (col_row == lane_row) & (lane_place < jnp.maximum(col_len, 1))
    query_ok = col_place < col_len

    def span_column(r, start, count):
        flags = jnp.broadcast_to(span_ref[r : r + 1, :], (count, length))
        place = lax.broadcasted_iota(jnp.int32, (count, length), 0) + start
        lane = lax.broadcasted_iota(jnp.int32, (count, length), 1)
        return jnp.sum(
            jnp.where((place == lane) & (flags == 1), 1.0, 0.0), axis=1, keepdims=True
        )

    span_natural = [span_column(r, 0, length) for r in range(rows)]
    denoiser_col = [jnp.full((1, 1), denoiser_ref[r], jnp.int32) for r in range(rows)]

    load_inputs.wait()
    norm_width = width // NORM_CHUNKS
    squares = jnp.zeros((total, 1), F32)
    for chunk in range(NORM_CHUNKS):
        columns = pl.ds(chunk * norm_width, norm_width)
        sentinel = sentinel_ref[:, columns].astype(F32)
        table = table_ref[:, columns].astype(F32)
        pieces = []
        for r in range(rows):
            mode_row = jnp.zeros((1, norm_width), F32)
            for mode in range(mode_count):
                mode_row = jnp.where(denoiser_col[r] == mode, table[mode : mode + 1], mode_row)
            plain = inputs_ref[r, :, columns].astype(F32) + mode_row
            pieces.append(jnp.where(span_natural[r] > 0.5, sentinel, plain).astype(BF16))
        shaped = matmul(permute, jnp.concatenate(pieces, axis=0))
        normed_ref[:, columns] = shaped
        squares += jnp.sum(shaped * shaped, axis=1, keepdims=True)
    inv_rms = lax.rsqrt(squares * (1.0 / width) + 1e-06)
    for chunk in range(NORM_CHUNKS):
        columns = pl.ds(chunk * norm_width, norm_width)
        normed = normed_ref[:, columns] * inv_rms
        normed_ref[:, columns] = normed
        normed_b_ref[:, columns] = normed.astype(BF16)

    pl.semaphore_wait(barrier, 2 + mp_count - 1)
    cot_copies = []
    for at, (slot, home) in enumerate(((rows, left), (rows + 1, right))):
        copy = pltpu.make_async_remote_copy(
            src_ref=cot_hbm.at[slot],
            dst_ref=cot_recv.at[at],
            send_sem=cot_send_sem.at[at],
            recv_sem=cot_recv_sem.at[at],
            device_id={"dp": home},
            device_id_type=MESH,
        )
        copy.start()
        cot_copies.append(copy)

    projected = []
    for which in range(3):
        result = jnp.zeros((total, head), F32)
        for chunk in range(FORWARD_CHUNKS):
            loads[which * FORWARD_CHUNKS + chunk].wait()
            piece = pl.ds(chunk * depth, depth)
            result += matmul(normed_b_ref[:, piece], weights[which, piece, :])
        projected.append(result)
    query, key, value = [result.astype(BF16) for result in projected]

    factor = 1.0 / math.sqrt(head)
    scores = jnp.where(key_ok, matmul(query, key, NT) * factor, -jnp.inf)
    exp_scores = jnp.exp(scores - jnp.max(scores, axis=1, keepdims=True))
    soft = exp_scores / jnp.sum(exp_scores, axis=1, keepdims=True)
    soft_b = soft.astype(BF16)
    context = jnp.where(query_ok, matmul(soft_b, value), 0.0).astype(BF16)
    context = matmul(permute, context, TN)

    def moves(r, offset):
        return jnp.full((1, 1), move_ref[r], jnp.int32) == offset

    for at, offset in enumerate((1, -1)):
        leaving = jnp.zeros((length, head), F32)
        for r in range(rows):
            leaving = jnp.where(moves(r, offset), context[r * length : (r + 1) * length], leaving)
        ctx_send[at] = leaving.astype(BF16)
    ctx_copies = []
    for at, (slot, target) in enumerate(((rows, right), (rows + 1, left))):
        copy = pltpu.make_async_remote_copy(
            src_ref=ctx_send.at[at],
            dst_ref=context_ref.at[slot],
            send_sem=ctx_send_sem.at[at],
            recv_sem=ctx_recv_sem.at[at],
            device_id={"dp": target},
            device_id_type=MESH,
        )
        copy.start()
        ctx_copies.append(copy)
    for r in range(rows):
        own = jnp.where(moves(r, 0), context[r * length : (r + 1) * length], 0.0)
        context_ref[r] = own.astype(BF16)

    load_cot.wait()
    for copy in cot_copies:
        copy.wait()
    from_right = cot_recv[0].astype(F32)
    from_left = cot_recv[1].astype(F32)
    pieces = []
    for r in range(rows):
        moved = jnp.where(moves(r, 1), from_right, from_left)
        pieces.append(jnp.where(moves(r, 0), cot_ref[r].astype(F32), moved).astype(BF16))
    grad_out = matmul(permute, jnp.concatenate(pieces, axis=0))
    grad_out = jnp.where(query_ok, grad_out, 0.0).astype(BF16)

    grad_value = matmul(soft_b, grad_out, TN).astype(BF16)
    grad_soft = matmul(grad_out, value, NT)
    row_inner = jnp.sum(soft * grad_soft, axis=1, keepdims=True)
    grad_scores = (soft * (grad_soft - row_inner) * factor).astype(BF16)
    grad_query = matmul(grad_scores, key).astype(BF16)
    grad_key = matmul(grad_scores, query, TN).astype(BF16)
    gradients = (grad_query, grad_key, grad_value)
    inner = jnp.zeros((total, 1), F32)
    for gradient, result in zip(gradients, projected):
        inner += jnp.sum(gradient.astype(F32) * result, axis=1, keepdims=True)
    inner = inner * (1.0 / width)

    back_width = width // BACK_CHUNKS
    half = back_width // 2
    part_copies = []
    for chunk in range(BACK_CHUNKS):
        piece = pl.ds(chunk * back_width, back_width)
        head_grad = matmul(gradients[0], weights[0, piece, :], NT)
        head_grad += matmul(gradients[1], weights[1, piece, :], NT)
        head_grad += matmul(gradients[2], weights[2, piece, :], NT)
        head_part = (head_grad - normed_ref[:, piece] * inner) * inv_rms
        for s in range(mp_count):
            block = head_part[s * seg_total : (s + 1) * seg_total]
            stacked = jnp.concatenate([block[:, :half], block[:, half:]], axis=0)
            part_send[chunk, s] = stacked.astype(BF16)
        copies = []
        for step in range(1, mp_count):
            peer = lax.rem(my_mp + step, mp_count)
            copy = pltpu.make_async_remote_copy(
                src_ref=part_send.at[chunk, peer],
                dst_ref=part_recv.at[chunk, step - 1],
                send_sem=part_send_sem.at[chunk, step - 1],
                recv_sem=part_recv_sem.at[chunk, step - 1],
                device_id={"mp": peer},
                device_id_type=MESH,
            )
            copy.start()
            copies.append(copy)
        part_copies.append(copies)

    span_own = jnp.concatenate(
        [span_column(r, my_mp * seg, seg) for r in range(rows)], axis=0
    )
    for chunk in range(BACK_CHUNKS):
        summed = part_send[chunk, my_mp].astype(F32)
        for step in range(1, mp_count):
            part_copies[chunk][step - 1].wait_recv()
            summed += part_recv[chunk, step - 1].astype(F32)
        for part in range(2):
            block = jnp.where(
                span_own > 0.5, 0.0, summed[part * seg_total : (part + 1) * seg_total]
            ).astype(BF16)
            columns = pl.ds(chunk * back_width + part * half, half)
            for r in range(rows):
                grad_ref[r, :, columns] = block[r * seg : (r + 1) * seg]

    for copies in part_copies:
        for copy in copies:
            copy.wait_send()
    for copy in ctx_copies:
        copy.wait()


def shards(
    inputs,
    denoiser,
    span_mask,
    lengths,
    move_plan,
    mode_table,
    sentinel,
    w_query,
    w_key,
    w_value,
    cotangent,
):
    rows, length, width = inputs.shape
    head = w_query.shape[1]
    dp_count = lax.axis_size("dp")
    mp_count = lax.axis_size("mp")
    seg = length // mp_count
    total = rows * length
    block = (2 * rows * seg, width // BACK_CHUNKS // 2)
    smem = pl.BlockSpec(memory_space=pltpu.SMEM)
    vmem = pl.BlockSpec(memory_space=pltpu.VMEM)
    anywhere = pl.BlockSpec(memory_space=pltpu.HBM)
    dma = pltpu.SemaphoreType.DMA
    return pl.pallas_call(
        functools.partial(kernel, dp_count, mp_count),
        out_shape=(
            jax.ShapeDtypeStruct(cotangent.shape, BF16),
            jax.ShapeDtypeStruct((rows, seg, width), BF16),
        ),
        in_specs=[smem, smem, smem, vmem, vmem, vmem] + [anywhere] * 5,
        out_specs=(vmem, vmem),
        scratch_shapes=[
            pltpu.VMEM((rows, length, width), BF16),
            pltpu.VMEM((rows, length, head), BF16),
            pltpu.VMEM((3, width, head), BF16),
            pltpu.VMEM((total, width), F32),
            pltpu.VMEM((total, width), BF16),
            pltpu.VMEM((2, length, head), BF16),
            pltpu.VMEM((2, length, head), BF16),
            pltpu.VMEM((BACK_CHUNKS, mp_count) + block, BF16),
            pltpu.VMEM((BACK_CHUNKS, mp_count - 1) + block, BF16),
            dma((2,)),
            dma((3, FORWARD_CHUNKS)),
            dma((2,)),
            dma((2,)),
            dma((2,)),
            dma((2,)),
            dma((BACK_CHUNKS, mp_count - 1)),
            dma((BACK_CHUNKS, mp_count - 1)),
        ],
        compiler_params=pltpu.CompilerParams(
            collective_id=0, has_side_effects=True, vmem_limit_bytes=48 * 1024 * 1024
        ),
        cost_estimate=pl.CostEstimate(
            flops=4 * total * width * 3 * head,
            bytes_accessed=2 * 3 * width * head + 4 * total * width,
            transcendentals=total * total,
        ),
    )(
        denoiser,
        lengths,
        move_plan,
        span_mask,
        mode_table,
        sentinel.reshape(1, width),
        inputs,
        cotangent,
        w_query,
        w_key,
        w_value,
    )


def solution(mesh):
    return jax.shard_map(
        shards,
        mesh=mesh,
        in_specs=(
            P("dp", None, None),
            P("dp"),
            P("dp", None),
            P("dp"),
            P("dp"),
            P(),
            P(),
            P(None, "mp"),
            P(None, "mp"),
            P(None, "mp"),
            P("dp", None, "mp"),
        ),
        out_specs=(P("dp", None, "mp"), P("dp", "mp", None)),
        check_vma=False,
    )
```

```python
import functools
import math

import jax
import jax.numpy as jnp
from jax import lax
from jax.experimental import pallas as pl
from jax.experimental.pallas import tpu as pltpu
from jax.sharding import PartitionSpec as P

MESH = pl.DeviceIdType.MESH
F32 = jnp.float32
BF16 = jnp.bfloat16
NT = (((1,), (1,)), ((), ()))
TN = (((0,), (0,)), ((), ()))
NN = (((1,), (0,)), ((), ()))

FORWARD_CHUNKS = 4
BACK_CHUNKS = 4
NORM_CHUNKS = 4
LANES = 128


def matmul(a, b, dims=NN):
    return lax.dot_general(a, b, dims, preferred_element_type=F32)


def kernel(
    dp_count,
    mp_count,
    denoiser_hbm,
    lengths_hbm,
    move_hbm,
    span_hbm,
    table_hbm,
    sentinel_hbm,
    inputs_hbm,
    cot_hbm,
    wq_hbm,
    wk_hbm,
    wv_hbm,
    context_ref,
    grad_ref,
    denoiser_ref,
    lengths_ref,
    move_ref,
    span_ref,
    table_ref,
    sentinel_ref,
    inputs_ref,
    cot_ref,
    weights,
    normed_ref,
    normed_b_ref,
    cot_recv,
    ctx_send,
    part_send,
    part_recv,
    small_sem,
    in_sem,
    w_sem,
    cot_send_sem,
    cot_recv_sem,
    ctx_send_sem,
    ctx_recv_sem,
    part_send_sem,
    part_recv_sem,
):
    rows, length, width = inputs_ref.shape
    head = weights.shape[2]
    seg = length // mp_count
    total = rows * length
    seg_total = rows * seg
    mode_count = table_ref.shape[0]
    my_dp = lax.axis_index("dp")
    my_mp = lax.axis_index("mp")
    right = lax.rem(my_dp + 1, dp_count)
    left = lax.rem(my_dp + dp_count - 1, dp_count)

    barrier = pltpu.get_barrier_semaphore()
    for neighbour in (left, right):
        pl.semaphore_signal(barrier, inc=1, device_id={"dp": neighbour}, device_id_type=MESH)
    for step in range(1, mp_count):
        pl.semaphore_signal(
            barrier,
            inc=1,
            device_id={"mp": lax.rem(my_mp + step, mp_count)},
            device_id_type=MESH,
        )

    small_loads = []
    for at, (source, target) in enumerate(
        (
            (denoiser_hbm, denoiser_ref),
            (lengths_hbm, lengths_ref),
            (move_hbm, move_ref),
            (span_hbm, span_ref),
            (table_hbm, table_ref),
            (sentinel_hbm, sentinel_ref),
        )
    ):
        load = pltpu.make_async_copy(source, target, small_sem.at[at])
        load.start()
        small_loads.append(load)
    load_inputs = pltpu.make_async_copy(inputs_hbm, inputs_ref, in_sem.at[0])
    load_inputs.start()
    load_cot = pltpu.make_async_copy(cot_hbm.at[pl.ds(0, rows)], cot_ref, in_sem.at[1])
    load_cot.start()
    depth = width // FORWARD_CHUNKS
    loads = []
    for which, source in enumerate((wq_hbm, wk_hbm, wv_hbm)):
        for chunk in range(FORWARD_CHUNKS):
            piece = pl.ds(chunk * depth, depth)
            load = pltpu.make_async_copy(
                source.at[piece], weights.at[which, piece], w_sem.at[which, chunk]
            )
            load.start()
            loads.append(load)

    for load in small_loads:
        load.wait()

    def split(index):
        row = lax.rem(lax.div(index, seg), rows)
        place = lax.div(index, seg_total) * seg + lax.rem(index, seg)
        return row, place

    def per_row(row, ref):
        value = jnp.zeros_like(row)
        for r in range(rows):
            value = jnp.where(row == r, ref[r], value)
        return value

    col_row, col_place = split(lax.broadcasted_iota(jnp.int32, (total, 1), 0))
    lane_row, lane_place = split(lax.broadcasted_iota(jnp.int32, (1, total), 1))
    natural_lane = lax.broadcasted_iota(jnp.int32, (total, total), 1)
    permute = (natural_lane == col_row * length + col_place).astype(F32).astype(BF16)
    col_len = per_row(col_row, lengths_ref)
    key_ok = (col_row == lane_row) & (lane_place < jnp.maximum(col_len, 1))
    query_ok = col_place < col_len

    def span_column(r, start, count):
        flags = jnp.broadcast_to(span_ref[r : r + 1, :], (count, length))
        place = lax.broadcasted_iota(jnp.int32, (count, length), 0) + start
        lane = lax.broadcasted_iota(jnp.int32, (count, length), 1)
        return jnp.sum(
            jnp.where((place == lane) & (flags == 1), 1.0, 0.0), axis=1, keepdims=True
        )

    span_natural = [span_column(r, 0, length) for r in range(rows)]
    denoiser_col = [jnp.full((1, 1), denoiser_ref[r], jnp.int32) for r in range(rows)]

    load_inputs.wait()
    norm_width = width // NORM_CHUNKS
    squares = jnp.zeros((total, 1), F32)
    for chunk in range(NORM_CHUNKS):
        columns = pl.ds(chunk * norm_width, norm_width)
        lines = norm_width // LANES
        lines_f32 = sentinel_ref[pl.ds(chunk * lines, lines), :].astype(F32)
        sentinel = jnp.concatenate([lines_f32[i : i + 1] for i in range(lines)], axis=1)
        table = table_ref[:, columns].astype(F32)
        pieces = []
        for r in range(rows):
            mode_row = jnp.zeros((1, norm_width), F32)
            for mode in range(mode_count):
                mode_row = jnp.where(denoiser_col[r] == mode, table[mode : mode + 1], mode_row)
            plain = inputs_ref[r, :, columns].astype(F32) + mode_row
            pieces.append(jnp.where(span_natural[r] > 0.5, sentinel, plain).astype(BF16))
        shaped = matmul(permute, jnp.concatenate(pieces, axis=0))
        normed_ref[:, columns] = shaped
        squares += jnp.sum(shaped * shaped, axis=1, keepdims=True)
    inv_rms = lax.rsqrt(squares * (1.0 / width) + 1e-06)
    for chunk in range(NORM_CHUNKS):
        columns = pl.ds(chunk * norm_width, norm_width)
        normed = normed_ref[:, columns] * inv_rms
        normed_ref[:, columns] = normed
        normed_b_ref[:, columns] = normed.astype(BF16)

    pl.semaphore_wait(barrier, 2 + mp_count - 1)
    cot_copies = []
    for at, (slot, home) in enumerate(((rows, left), (rows + 1, right))):
        copy = pltpu.make_async_remote_copy(
            src_ref=cot_hbm.at[slot],
            dst_ref=cot_recv.at[at],
            send_sem=cot_send_sem.at[at],
            recv_sem=cot_recv_sem.at[at],
            device_id={"dp": home},
            device_id_type=MESH,
        )
        copy.start()
        cot_copies.append(copy)

    projected = []
    for which in range(3):
        result = jnp.zeros((total, head), F32)
        for chunk in range(FORWARD_CHUNKS):
            loads[which * FORWARD_CHUNKS + chunk].wait()
            piece = pl.ds(chunk * depth, depth)
            result += matmul(normed_b_ref[:, piece], weights[which, piece, :])
        projected.append(result)
    query, key, value = [result.astype(BF16) for result in projected]

    factor = 1.0 / math.sqrt(head)
    scores = jnp.where(key_ok, matmul(query, key, NT) * factor, -jnp.inf)
    exp_scores = jnp.exp(scores - jnp.max(scores, axis=1, keepdims=True))
    soft = exp_scores / jnp.sum(exp_scores, axis=1, keepdims=True)
    soft_b = soft.astype(BF16)
    def moves(r, offset):
        return jnp.full((1, 1), move_ref[r], jnp.int32) == offset

    load_cot.wait()
    for copy in cot_copies:
        copy.wait()
    from_right = cot_recv[0].astype(F32)
    from_left = cot_recv[1].astype(F32)
    pieces = []
    for r in range(rows):
        moved = jnp.where(moves(r, 1), from_right, from_left)
        pieces.append(jnp.where(moves(r, 0), cot_ref[r].astype(F32), moved).astype(BF16))
    grad_out = matmul(permute, jnp.concatenate(pieces, axis=0))
    grad_out = jnp.where(query_ok, grad_out, 0.0).astype(BF16)

    grad_value = matmul(soft_b, grad_out, TN).astype(BF16)
    grad_soft = matmul(grad_out, value, NT)
    row_inner = jnp.sum(soft * grad_soft, axis=1, keepdims=True)
    grad_scores = (soft * (grad_soft - row_inner) * factor).astype(BF16)
    grad_query = matmul(grad_scores, key).astype(BF16)
    grad_key = matmul(grad_scores, query, TN).astype(BF16)
    gradients = (grad_query, grad_key, grad_value)
    inner = jnp.zeros((total, 1), F32)
    for gradient, result in zip(gradients, projected):
        inner += jnp.sum(gradient.astype(F32) * result, axis=1, keepdims=True)
    inner = inner * (1.0 / width)

    back_width = width // BACK_CHUNKS
    half = back_width // 2
    part_copies = []
    for chunk in range(BACK_CHUNKS):
        piece = pl.ds(chunk * back_width, back_width)
        head_grad = matmul(gradients[0], weights[0, piece, :], NT)
        head_grad += matmul(gradients[1], weights[1, piece, :], NT)
        head_grad += matmul(gradients[2], weights[2, piece, :], NT)
        head_part = (head_grad - normed_ref[:, piece] * inner) * inv_rms
        for s in range(mp_count):
            block = head_part[s * seg_total : (s + 1) * seg_total]
            stacked = jnp.concatenate([block[:, :half], block[:, half:]], axis=0)
            part_send[chunk, s] = stacked.astype(BF16)
        copies = []
        for step in range(1, mp_count):
            peer = lax.rem(my_mp + step, mp_count)
            copy = pltpu.make_async_remote_copy(
                src_ref=part_send.at[chunk, peer],
                dst_ref=part_recv.at[chunk, step - 1],
                send_sem=part_send_sem.at[chunk, step - 1],
                recv_sem=part_recv_sem.at[chunk, step - 1],
                device_id={"mp": peer},
                device_id_type=MESH,
            )
            copy.start()
            copies.append(copy)
        part_copies.append(copies)

    context = jnp.where(query_ok, matmul(soft_b, value), 0.0).astype(BF16)
    context = matmul(permute, context, TN)

    for at, offset in enumerate((1, -1)):
        leaving = jnp.zeros((length, head), F32)
        for r in range(rows):
            leaving = jnp.where(moves(r, offset), context[r * length : (r + 1) * length], leaving)
        ctx_send[at] = leaving.astype(BF16)
    ctx_copies = []
    for at, (slot, target) in enumerate(((rows, right), (rows + 1, left))):
        copy = pltpu.make_async_remote_copy(
            src_ref=ctx_send.at[at],
            dst_ref=context_ref.at[slot],
            send_sem=ctx_send_sem.at[at],
            recv_sem=ctx_recv_sem.at[at],
            device_id={"dp": target},
            device_id_type=MESH,
        )
        copy.start()
        ctx_copies.append(copy)
    for r in range(rows):
        own = jnp.where(moves(r, 0), context[r * length : (r + 1) * length], 0.0)
        context_ref[r] = own.astype(BF16)

    span_own = jnp.concatenate(
        [span_column(r, my_mp * seg, seg) for r in range(rows)], axis=0
    )
    for chunk in range(BACK_CHUNKS):
        summed = part_send[chunk, my_mp].astype(F32)
        for step in range(1, mp_count):
            part_copies[chunk][step - 1].wait_recv()
            summed += part_recv[chunk, step - 1].astype(F32)
        for part in range(2):
            block = jnp.where(
                span_own > 0.5, 0.0, summed[part * seg_total : (part + 1) * seg_total]
            ).astype(BF16)
            columns = pl.ds(chunk * back_width + part * half, half)
            for r in range(rows):
                grad_ref[r, :, columns] = block[r * seg : (r + 1) * seg]

    for copies in part_copies:
        for copy in copies:
            copy.wait_send()
    for copy in ctx_copies:
        copy.wait()


def shards(
    inputs,
    denoiser,
    span_mask,
    lengths,
    move_plan,
    mode_table,
    sentinel,
    w_query,
    w_key,
    w_value,
    cotangent,
):
    rows, length, width = inputs.shape
    head = w_query.shape[1]
    dp_count = lax.axis_size("dp")
    mp_count = lax.axis_size("mp")
    seg = length // mp_count
    total = rows * length
    block = (2 * rows * seg, width // BACK_CHUNKS // 2)
    vmem = pl.BlockSpec(memory_space=pltpu.VMEM)
    anywhere = pl.BlockSpec(memory_space=pltpu.HBM)
    dma = pltpu.SemaphoreType.DMA
    return pl.pallas_call(
        functools.partial(kernel, dp_count, mp_count),
        out_shape=(
            jax.ShapeDtypeStruct(cotangent.shape, BF16),
            jax.ShapeDtypeStruct((rows, seg, width), BF16),
        ),
        in_specs=[anywhere] * 11,
        out_specs=(vmem, vmem),
        scratch_shapes=[
            pltpu.SMEM((rows,), jnp.int32),
            pltpu.SMEM((rows,), jnp.int32),
            pltpu.SMEM((rows,), jnp.int32),
            pltpu.VMEM((rows, length), jnp.int32),
            pltpu.VMEM(mode_table.shape, BF16),
            pltpu.VMEM((width // LANES, LANES), BF16),
            pltpu.VMEM((rows, length, width), BF16),
            pltpu.VMEM((rows, length, head), BF16),
            pltpu.VMEM((3, width, head), BF16),
            pltpu.VMEM((total, width), F32),
            pltpu.VMEM((total, width), BF16),
            pltpu.VMEM((2, length, head), BF16),
            pltpu.VMEM((2, length, head), BF16),
            pltpu.VMEM((BACK_CHUNKS, mp_count) + block, BF16),
            pltpu.VMEM((BACK_CHUNKS, mp_count - 1) + block, BF16),
            dma((6,)),
            dma((2,)),
            dma((3, FORWARD_CHUNKS)),
            dma((2,)),
            dma((2,)),
            dma((2,)),
            dma((2,)),
            dma((BACK_CHUNKS, mp_count - 1)),
            dma((BACK_CHUNKS, mp_count - 1)),
        ],
        compiler_params=pltpu.CompilerParams(
            collective_id=0, has_side_effects=True, vmem_limit_bytes=64 * 1024 * 1024
        ),
        cost_estimate=pl.CostEstimate(
            flops=4 * total * width * 3 * head,
            bytes_accessed=2 * 3 * width * head + 4 * total * width,
            transcendentals=total * total,
        ),
    )(
        denoiser,
        lengths,
        move_plan,
        span_mask,
        mode_table,
        sentinel.reshape(width // LANES, LANES),
        inputs,
        cotangent,
        w_query,
        w_key,
        w_value,
    )


def solution(mesh):
    return jax.shard_map(
        shards,
        mesh=mesh,
        in_specs=(
            P("dp", None, None),
            P("dp"),
            P("dp", None),
            P("dp"),
            P("dp"),
            P(),
            P(),
            P(None, "mp"),
            P(None, "mp"),
            P(None, "mp"),
            P("dp", None, "mp"),
        ),
        out_specs=(P("dp", None, "mp"), P("dp", "mp", None)),
        check_vma=False,
    )
```

```python
import functools
import math

import jax
import jax.numpy as jnp
from jax import lax
from jax.experimental import pallas as pl
from jax.experimental.pallas import tpu as pltpu
from jax.sharding import PartitionSpec as P

MESH = pl.DeviceIdType.MESH
F32 = jnp.float32
BF16 = jnp.bfloat16
NT = (((1,), (1,)), ((), ()))
TN = (((0,), (0,)), ((), ()))
NN = (((1,), (0,)), ((), ()))

FORWARD_CHUNKS = 4
BACK_CHUNKS = 4
NORM_CHUNKS = 4
LANES = 128


def matmul(a, b, dims=NN):
    return lax.dot_general(a, b, dims, preferred_element_type=F32)


def kernel(
    dp_count,
    mp_count,
    denoiser_hbm,
    lengths_hbm,
    move_hbm,
    span_hbm,
    table_hbm,
    sentinel_hbm,
    inputs_hbm,
    cot_hbm,
    wq_hbm,
    wk_hbm,
    wv_hbm,
    context_ref,
    grad_ref,
    denoiser_ref,
    lengths_ref,
    move_ref,
    span_ref,
    table_ref,
    sentinel_ref,
    inputs_ref,
    cot_ref,
    weights,
    normed_ref,
    normed_b_ref,
    cot_recv,
    ctx_send,
    part_send,
    part_recv,
    small_sem,
    in_sem,
    w_sem,
    cot_send_sem,
    cot_recv_sem,
    ctx_send_sem,
    ctx_recv_sem,
    part_send_sem,
    part_recv_sem,
):
    rows, length, width = inputs_ref.shape
    head = weights.shape[2]
    seg = length // mp_count
    total = rows * length
    seg_total = rows * seg
    mode_count = table_ref.shape[0]
    my_dp = lax.axis_index("dp")
    my_mp = lax.axis_index("mp")
    right = lax.rem(my_dp + 1, dp_count)
    left = lax.rem(my_dp + dp_count - 1, dp_count)

    barrier = pltpu.get_barrier_semaphore()
    for neighbour in (left, right):
        pl.semaphore_signal(barrier, inc=1, device_id={"dp": neighbour}, device_id_type=MESH)
    for step in range(1, mp_count):
        pl.semaphore_signal(
            barrier,
            inc=1,
            device_id={"mp": lax.rem(my_mp + step, mp_count)},
            device_id_type=MESH,
        )

    small_loads = []
    for at, (source, target) in enumerate(
        (
            (denoiser_hbm, denoiser_ref),
            (lengths_hbm, lengths_ref),
            (move_hbm, move_ref),
            (span_hbm, span_ref),
            (table_hbm, table_ref),
            (sentinel_hbm, sentinel_ref),
        )
    ):
        load = pltpu.make_async_copy(source, target, small_sem.at[at])
        load.start()
        small_loads.append(load)
    load_inputs = pltpu.make_async_copy(inputs_hbm, inputs_ref, in_sem.at[0])
    load_inputs.start()
    load_cot = pltpu.make_async_copy(cot_hbm.at[pl.ds(0, rows)], cot_ref, in_sem.at[1])
    load_cot.start()
    depth = width // FORWARD_CHUNKS
    loads = []
    for which, source in enumerate((wq_hbm, wk_hbm, wv_hbm)):
        for chunk in range(FORWARD_CHUNKS):
            piece = pl.ds(chunk * depth, depth)
            load = pltpu.make_async_copy(
                source.at[piece], weights.at[which, piece], w_sem.at[which, chunk]
            )
            load.start()
            loads.append(load)

    for load in small_loads:
        load.wait()

    def split(index):
        row = lax.rem(lax.div(index, seg), rows)
        place = lax.div(index, seg_total) * seg + lax.rem(index, seg)
        return row, place

    def per_row(row, ref):
        value = jnp.zeros_like(row)
        for r in range(rows):
            value = jnp.where(row == r, ref[r], value)
        return value

    col_row, col_place = split(lax.broadcasted_iota(jnp.int32, (total, 1), 0))
    lane_row, lane_place = split(lax.broadcasted_iota(jnp.int32, (1, total), 1))
    natural_lane = lax.broadcasted_iota(jnp.int32, (total, total), 1)
    permute = (natural_lane == col_row * length + col_place).astype(F32).astype(BF16)
    col_len = per_row(col_row, lengths_ref)
    key_ok = (col_row == lane_row) & (lane_place < jnp.maximum(col_len, 1))
    query_ok = col_place < col_len

    def span_column(r, start, count):
        flags = jnp.broadcast_to(span_ref[r : r + 1, :], (count, length))
        place = lax.broadcasted_iota(jnp.int32, (count, length), 0) + start
        lane = lax.broadcasted_iota(jnp.int32, (count, length), 1)
        return jnp.sum(
            jnp.where((place == lane) & (flags == 1), 1.0, 0.0), axis=1, keepdims=True
        )

    span_natural = [span_column(r, 0, length) for r in range(rows)]
    denoiser_col = [jnp.full((1, 1), denoiser_ref[r], jnp.int32) for r in range(rows)]

    load_inputs.wait()
    norm_width = width // NORM_CHUNKS
    squares = jnp.zeros((total, 1), F32)
    for chunk in range(NORM_CHUNKS):
        columns = pl.ds(chunk * norm_width, norm_width)
        lines = norm_width // LANES
        lines_f32 = sentinel_ref[pl.ds(chunk * lines, lines), :].astype(F32)
        sentinel = jnp.concatenate([lines_f32[i : i + 1] for i in range(lines)], axis=1)
        table = table_ref[:, columns].astype(F32)
        pieces = []
        for r in range(rows):
            mode_row = jnp.zeros((1, norm_width), F32)
            for mode in range(mode_count):
                mode_row = jnp.where(denoiser_col[r] == mode, table[mode : mode + 1], mode_row)
            plain = inputs_ref[r, :, columns].astype(F32) + mode_row
            pieces.append(jnp.where(span_natural[r] > 0.5, sentinel, plain).astype(BF16))
        shaped = matmul(permute, jnp.concatenate(pieces, axis=0))
        normed_ref[:, columns] = shaped
        squares += jnp.sum(shaped * shaped, axis=1, keepdims=True)
    inv_rms = lax.rsqrt(squares * (1.0 / width) + 1e-06)
    for chunk in range(NORM_CHUNKS):
        columns = pl.ds(chunk * norm_width, norm_width)
        normed = normed_ref[:, columns] * inv_rms
        normed_ref[:, columns] = normed
        normed_b_ref[:, columns] = normed.astype(BF16)

    pl.semaphore_wait(barrier, 2 + mp_count - 1)
    cot_copies = []
    for at, (slot, home) in enumerate(((rows, left), (rows + 1, right))):
        copy = pltpu.make_async_remote_copy(
            src_ref=cot_hbm.at[slot],
            dst_ref=cot_recv.at[at],
            send_sem=cot_send_sem.at[at],
            recv_sem=cot_recv_sem.at[at],
            device_id={"dp": home},
            device_id_type=MESH,
        )
        copy.start()
        cot_copies.append(copy)

    projected = []
    for which in range(3):
        result = jnp.zeros((total, head), F32)
        for chunk in range(FORWARD_CHUNKS):
            loads[which * FORWARD_CHUNKS + chunk].wait()
            piece = pl.ds(chunk * depth, depth)
            result += matmul(normed_b_ref[:, piece], weights[which, piece, :])
        projected.append(result)
    query, key, value = [result.astype(BF16) for result in projected]

    factor = 1.0 / math.sqrt(head)
    scores = jnp.where(key_ok, matmul(query, key, NT) * factor, -jnp.inf)
    exp_scores = jnp.exp(scores - jnp.max(scores, axis=1, keepdims=True))
    soft = exp_scores / jnp.sum(exp_scores, axis=1, keepdims=True)
    soft_b = soft.astype(BF16)
    def moves(r, offset):
        return jnp.full((1, 1), move_ref[r], jnp.int32) == offset

    load_cot.wait()
    for copy in cot_copies:
        copy.wait()
    from_right = cot_recv[0].astype(F32)
    from_left = cot_recv[1].astype(F32)
    pieces = []
    for r in range(rows):
        moved = jnp.where(moves(r, 1), from_right, from_left)
        pieces.append(jnp.where(moves(r, 0), cot_ref[r].astype(F32), moved).astype(BF16))
    grad_out = matmul(permute, jnp.concatenate(pieces, axis=0))
    grad_out = jnp.where(query_ok, grad_out, 0.0).astype(BF16)

    grad_value = matmul(soft_b, grad_out, TN).astype(BF16)
    grad_soft = matmul(grad_out, value, NT)
    row_inner = jnp.sum(soft * grad_soft, axis=1, keepdims=True)
    grad_scores = (soft * (grad_soft - row_inner) * factor).astype(BF16)
    grad_query = matmul(grad_scores, key).astype(BF16)
    grad_key = matmul(grad_scores, query, TN).astype(BF16)
    gradients = (grad_query, grad_key, grad_value)
    inner = jnp.zeros((total, 1), F32)
    for gradient, result in zip(gradients, projected):
        inner += jnp.sum(gradient.astype(F32) * result, axis=1, keepdims=True)
    inner = inner * (1.0 / width)

    back_width = width // BACK_CHUNKS
    half = back_width // 2
    part_copies = []
    for chunk in range(BACK_CHUNKS):
        piece = pl.ds(chunk * back_width, back_width)
        head_grad = matmul(gradients[0], weights[0, piece, :], NT)
        head_grad += matmul(gradients[1], weights[1, piece, :], NT)
        head_grad += matmul(gradients[2], weights[2, piece, :], NT)
        head_part = (head_grad - normed_ref[:, piece] * inner) * inv_rms
        for s in range(mp_count):
            block = head_part[s * seg_total : (s + 1) * seg_total]
            stacked = jnp.concatenate([block[:, :half], block[:, half:]], axis=0)
            part_send[chunk, s] = stacked.astype(BF16)
        copies = []
        for step in range(1, mp_count):
            peer = lax.rem(my_mp + step, mp_count)
            copy = pltpu.make_async_remote_copy(
                src_ref=part_send.at[chunk, peer],
                dst_ref=part_recv.at[chunk, step - 1],
                send_sem=part_send_sem.at[chunk, step - 1],
                recv_sem=part_recv_sem.at[chunk, step - 1],
                device_id={"mp": peer},
                device_id_type=MESH,
            )
            copy.start()
            copies.append(copy)
        part_copies.append(copies)

    context = jnp.where(query_ok, matmul(soft_b, value), 0.0).astype(BF16)
    context = matmul(permute, context, TN)

    for at, offset in enumerate((1, -1)):
        leaving = jnp.zeros((length, head), F32)
        for r in range(rows):
            leaving = jnp.where(moves(r, offset), context[r * length : (r + 1) * length], leaving)
        ctx_send[at] = leaving.astype(BF16)
    ctx_copies = []
    for at, (slot, target) in enumerate(((rows, right), (rows + 1, left))):
        copy = pltpu.make_async_remote_copy(
            src_ref=ctx_send.at[at],
            dst_ref=context_ref.at[slot],
            send_sem=ctx_send_sem.at[at],
            recv_sem=ctx_recv_sem.at[at],
            device_id={"dp": target},
            device_id_type=MESH,
        )
        copy.start()
        ctx_copies.append(copy)
    for r in range(rows):
        own = jnp.where(moves(r, 0), context[r * length : (r + 1) * length], 0.0)
        context_ref[r] = own.astype(BF16)

    span_own = jnp.concatenate(
        [span_column(r, my_mp * seg, seg) for r in range(rows)], axis=0
    )
    for chunk in range(BACK_CHUNKS):
        summed = part_send[chunk, my_mp].astype(F32)
        for step in range(1, mp_count):
            part_copies[chunk][step - 1].wait_recv()
            summed += part_recv[chunk, step - 1].astype(F32)
        for part in range(2):
            block = jnp.where(
                span_own > 0.5, 0.0, summed[part * seg_total : (part + 1) * seg_total]
            ).astype(BF16)
            columns = pl.ds(chunk * back_width + part * half, half)
            for r in range(rows):
                grad_ref[r, :, columns] = block[r * seg : (r + 1) * seg]

    for copies in part_copies:
        for copy in copies:
            copy.wait_send()
    for copy in ctx_copies:
        copy.wait()


def shards(
    inputs,
    denoiser,
    span_mask,
    lengths,
    move_plan,
    mode_table,
    sentinel,
    w_query,
    w_key,
    w_value,
    cotangent,
):
    rows, length, width = inputs.shape
    head = w_query.shape[1]
    dp_count = lax.axis_size("dp")
    mp_count = lax.axis_size("mp")
    seg = length // mp_count
    total = rows * length
    block = (2 * rows * seg, width // BACK_CHUNKS // 2)
    vmem = pl.BlockSpec(memory_space=pltpu.VMEM)
    anywhere = pl.BlockSpec(memory_space=pltpu.HBM)
    dma = pltpu.SemaphoreType.DMA
    return pl.pallas_call(
        functools.partial(kernel, dp_count, mp_count),
        out_shape=(
            pltpu.VMEM(cotangent.shape, BF16),
            pltpu.VMEM((rows, seg, width), BF16),
        ),
        in_specs=[anywhere] * 11,
        out_specs=(vmem, vmem),
        scratch_shapes=[
            pltpu.SMEM((rows,), jnp.int32),
            pltpu.SMEM((rows,), jnp.int32),
            pltpu.SMEM((rows,), jnp.int32),
            pltpu.VMEM((rows, length), jnp.int32),
            pltpu.VMEM(mode_table.shape, BF16),
            pltpu.VMEM((width // LANES, LANES), BF16),
            pltpu.VMEM((rows, length, width), BF16),
            pltpu.VMEM((rows, length, head), BF16),
            pltpu.VMEM((3, width, head), BF16),
            pltpu.VMEM((total, width), F32),
            pltpu.VMEM((total, width), BF16),
            pltpu.VMEM((2, length, head), BF16),
            pltpu.VMEM((2, length, head), BF16),
            pltpu.VMEM((BACK_CHUNKS, mp_count) + block, BF16),
            pltpu.VMEM((BACK_CHUNKS, mp_count - 1) + block, BF16),
            dma((6,)),
            dma((2,)),
            dma((3, FORWARD_CHUNKS)),
            dma((2,)),
            dma((2,)),
            dma((2,)),
            dma((2,)),
            dma((BACK_CHUNKS, mp_count - 1)),
            dma((BACK_CHUNKS, mp_count - 1)),
        ],
        compiler_params=pltpu.CompilerParams(
            collective_id=0, has_side_effects=True, vmem_limit_bytes=48 * 1024 * 1024
        ),
        cost_estimate=pl.CostEstimate(
            flops=4 * total * width * 3 * head,
            bytes_accessed=2 * 3 * width * head + 4 * total * width,
            transcendentals=total * total,
        ),
    )(
        *[
            pltpu.with_memory_space_constraint(operand, pltpu.HBM)
            for operand in (
                denoiser,
                lengths,
                move_plan,
                span_mask,
                mode_table,
                sentinel.reshape(width // LANES, LANES),
                inputs,
                cotangent,
                w_query,
                w_key,
                w_value,
            )
        ]
    )


def solution(mesh):
    return jax.shard_map(
        shards,
        mesh=mesh,
        in_specs=(
            P("dp", None, None),
            P("dp"),
            P("dp", None),
            P("dp"),
            P("dp"),
            P(),
            P(),
            P(None, "mp"),
            P(None, "mp"),
            P(None, "mp"),
            P("dp", None, "mp"),
        ),
        out_specs=(P("dp", None, "mp"), P("dp", "mp", None)),
        check_vma=False,
    )
```

```python
import functools
import math

import jax
import jax.numpy as jnp
from jax import lax
from jax.experimental import pallas as pl
from jax.experimental.pallas import tpu as pltpu
from jax.sharding import PartitionSpec as P

MESH = pl.DeviceIdType.MESH
F32 = jnp.float32
BF16 = jnp.bfloat16
NT = (((1,), (1,)), ((), ()))
TN = (((0,), (0,)), ((), ()))
NN = (((1,), (0,)), ((), ()))

FORWARD_CHUNKS = 4
BACK_CHUNKS = 8
NORM_CHUNKS = 4
LANES = 128


def matmul(a, b, dims=NN):
    return lax.dot_general(a, b, dims, preferred_element_type=F32)


def kernel(
    dp_count,
    mp_count,
    denoiser_hbm,
    lengths_hbm,
    move_hbm,
    span_hbm,
    table_hbm,
    sentinel_hbm,
    inputs_hbm,
    cot_hbm,
    wq_hbm,
    wk_hbm,
    wv_hbm,
    context_ref,
    grad_ref,
    denoiser_ref,
    lengths_ref,
    move_ref,
    span_ref,
    table_ref,
    sentinel_ref,
    inputs_ref,
    cot_ref,
    weights,
    normed_ref,
    normed_b_ref,
    cot_recv,
    ctx_send,
    part_send,
    part_recv,
    small_sem,
    in_sem,
    w_sem,
    cot_send_sem,
    cot_recv_sem,
    ctx_send_sem,
    ctx_recv_sem,
    part_send_sem,
    part_recv_sem,
):
    rows, length, width = inputs_ref.shape
    head = weights.shape[2]
    seg = length // mp_count
    total = rows * length
    seg_total = rows * seg
    mode_count = table_ref.shape[0]
    my_dp = lax.axis_index("dp")
    my_mp = lax.axis_index("mp")
    right = lax.rem(my_dp + 1, dp_count)
    left = lax.rem(my_dp + dp_count - 1, dp_count)

    barrier = pltpu.get_barrier_semaphore()
    for neighbour in (left, right):
        pl.semaphore_signal(barrier, inc=1, device_id={"dp": neighbour}, device_id_type=MESH)
    for step in range(1, mp_count):
        pl.semaphore_signal(
            barrier,
            inc=1,
            device_id={"mp": lax.rem(my_mp + step, mp_count)},
            device_id_type=MESH,
        )

    small_loads = []
    for at, (source, target) in enumerate(
        (
            (denoiser_hbm, denoiser_ref),
            (lengths_hbm, lengths_ref),
            (move_hbm, move_ref),
            (span_hbm, span_ref),
            (table_hbm, table_ref),
            (sentinel_hbm, sentinel_ref),
        )
    ):
        load = pltpu.make_async_copy(source, target, small_sem.at[at])
        load.start()
        small_loads.append(load)
    load_inputs = pltpu.make_async_copy(inputs_hbm, inputs_ref, in_sem.at[0])
    load_inputs.start()
    load_cot = pltpu.make_async_copy(cot_hbm.at[pl.ds(0, rows)], cot_ref, in_sem.at[1])
    load_cot.start()
    depth = width // FORWARD_CHUNKS
    loads = []
    for which, source in enumerate((wq_hbm, wk_hbm, wv_hbm)):
        for chunk in range(FORWARD_CHUNKS):
            piece = pl.ds(chunk * depth, depth)
            load = pltpu.make_async_copy(
                source.at[piece], weights.at[which, piece], w_sem.at[which, chunk]
            )
            load.start()
            loads.append(load)

    for load in small_loads:
        load.wait()

    def split(index):
        row = lax.rem(lax.div(index, seg), rows)
        place = lax.div(index, seg_total) * seg + lax.rem(index, seg)
        return row, place

    def per_row(row, ref):
        value = jnp.zeros_like(row)
        for r in range(rows):
            value = jnp.where(row == r, ref[r], value)
        return value

    col_row, col_place = split(lax.broadcasted_iota(jnp.int32, (total, 1), 0))
    lane_row, lane_place = split(lax.broadcasted_iota(jnp.int32, (1, total), 1))
    natural_lane = lax.broadcasted_iota(jnp.int32, (total, total), 1)
    permute = (natural_lane == col_row * length + col_place).astype(F32).astype(BF16)
    col_len = per_row(col_row, lengths_ref)
    key_ok = (col_row == lane_row) & (lane_place < jnp.maximum(col_len, 1))
    query_ok = col_place < col_len

    def span_column(r, start, count):
        flags = jnp.broadcast_to(span_ref[r : r + 1, :], (count, length))
        place = lax.broadcasted_iota(jnp.int32, (count, length), 0) + start
        lane = lax.broadcasted_iota(jnp.int32, (count, length), 1)
        return jnp.sum(
            jnp.where((place == lane) & (flags == 1), 1.0, 0.0), axis=1, keepdims=True
        )

    span_natural = [span_column(r, 0, length) for r in range(rows)]
    denoiser_col = [jnp.full((1, 1), denoiser_ref[r], jnp.int32) for r in range(rows)]

    load_inputs.wait()
    norm_width = width // NORM_CHUNKS
    squares = jnp.zeros((total, 1), F32)
    for chunk in range(NORM_CHUNKS):
        columns = pl.ds(chunk * norm_width, norm_width)
        lines = norm_width // LANES
        lines_f32 = sentinel_ref[pl.ds(chunk * lines, lines), :].astype(F32)
        sentinel = jnp.concatenate([lines_f32[i : i + 1] for i in range(lines)], axis=1)
        table = table_ref[:, columns].astype(F32)
        pieces = []
        for r in range(rows):
            mode_row = jnp.zeros((1, norm_width), F32)
            for mode in range(mode_count):
                mode_row = jnp.where(denoiser_col[r] == mode, table[mode : mode + 1], mode_row)
            plain = inputs_ref[r, :, columns].astype(F32) + mode_row
            pieces.append(jnp.where(span_natural[r] > 0.5, sentinel, plain).astype(BF16))
        shaped = matmul(permute, jnp.concatenate(pieces, axis=0))
        normed_ref[:, columns] = shaped
        squares += jnp.sum(shaped * shaped, axis=1, keepdims=True)
    inv_rms = lax.rsqrt(squares * (1.0 / width) + 1e-06)
    for chunk in range(NORM_CHUNKS):
        columns = pl.ds(chunk * norm_width, norm_width)
        normed = normed_ref[:, columns] * inv_rms
        normed_ref[:, columns] = normed
        normed_b_ref[:, columns] = normed.astype(BF16)

    pl.semaphore_wait(barrier, 2 + mp_count - 1)
    cot_copies = []
    for at, (slot, home) in enumerate(((rows, left), (rows + 1, right))):
        copy = pltpu.make_async_remote_copy(
            src_ref=cot_hbm.at[slot],
            dst_ref=cot_recv.at[at],
            send_sem=cot_send_sem.at[at],
            recv_sem=cot_recv_sem.at[at],
            device_id={"dp": home},
            device_id_type=MESH,
        )
        copy.start()
        cot_copies.append(copy)

    def project(which, chunk):
        piece = pl.ds(chunk * depth, depth)
        return matmul(normed_b_ref[:, piece], weights[which, piece, :])

    query_f32 = jnp.zeros((total, head), F32)
    key_f32 = jnp.zeros((total, head), F32)
    for chunk in range(FORWARD_CHUNKS):
        loads[chunk].wait()
        query_f32 += project(0, chunk)
    for chunk in range(FORWARD_CHUNKS):
        loads[FORWARD_CHUNKS + chunk].wait()
        key_f32 += project(1, chunk)
    for chunk in range(FORWARD_CHUNKS):
        loads[2 * FORWARD_CHUNKS + chunk].wait()
    load_cot.wait()
    for copy in cot_copies:
        copy.wait()

    query = query_f32.astype(BF16)
    key = key_f32.astype(BF16)
    factor = 1.0 / math.sqrt(head)
    scores = jnp.where(key_ok, matmul(query, key, NT) * factor, -jnp.inf)
    value_f32 = project(2, 0)
    for chunk in range(1, FORWARD_CHUNKS):
        value_f32 += project(2, chunk)
    exp_scores = jnp.exp(scores - jnp.max(scores, axis=1, keepdims=True))
    soft = exp_scores / jnp.sum(exp_scores, axis=1, keepdims=True)
    soft_b = soft.astype(BF16)
    value = value_f32.astype(BF16)
    projected = (query_f32, key_f32, value_f32)

    def moves(r, offset):
        return jnp.full((1, 1), move_ref[r], jnp.int32) == offset

    from_right = cot_recv[0].astype(F32)
    from_left = cot_recv[1].astype(F32)
    pieces = []
    for r in range(rows):
        moved = jnp.where(moves(r, 1), from_right, from_left)
        pieces.append(jnp.where(moves(r, 0), cot_ref[r].astype(F32), moved).astype(BF16))
    grad_out = matmul(permute, jnp.concatenate(pieces, axis=0))
    grad_out = jnp.where(query_ok, grad_out, 0.0).astype(BF16)

    grad_value = matmul(soft_b, grad_out, TN).astype(BF16)
    grad_soft = matmul(grad_out, value, NT)
    row_inner = jnp.sum(soft * grad_soft, axis=1, keepdims=True)
    grad_scores = (soft * (grad_soft - row_inner) * factor).astype(BF16)
    grad_query = matmul(grad_scores, key).astype(BF16)
    grad_key = matmul(grad_scores, query, TN).astype(BF16)
    gradients = (grad_query, grad_key, grad_value)
    inner = jnp.zeros((total, 1), F32)
    for gradient, result in zip(gradients, projected):
        inner += jnp.sum(gradient.astype(F32) * result, axis=1, keepdims=True)
    inner = inner * (1.0 / width)

    back_width = width // BACK_CHUNKS
    half = back_width // 2
    part_copies = []
    for chunk in range(BACK_CHUNKS):
        piece = pl.ds(chunk * back_width, back_width)
        head_grad = matmul(gradients[0], weights[0, piece, :], NT)
        head_grad += matmul(gradients[1], weights[1, piece, :], NT)
        head_grad += matmul(gradients[2], weights[2, piece, :], NT)
        head_part = (head_grad - normed_ref[:, piece] * inner) * inv_rms
        for s in range(mp_count):
            block = head_part[s * seg_total : (s + 1) * seg_total]
            stacked = jnp.concatenate([block[:, :half], block[:, half:]], axis=0)
            part_send[chunk, s] = stacked.astype(BF16)
        copies = []
        for step in range(1, mp_count):
            peer = lax.rem(my_mp + step, mp_count)
            copy = pltpu.make_async_remote_copy(
                src_ref=part_send.at[chunk, peer],
                dst_ref=part_recv.at[chunk, step - 1],
                send_sem=part_send_sem.at[chunk, step - 1],
                recv_sem=part_recv_sem.at[chunk, step - 1],
                device_id={"mp": peer},
                device_id_type=MESH,
            )
            copy.start()
            copies.append(copy)
        part_copies.append(copies)

    context = jnp.where(query_ok, matmul(soft_b, value), 0.0).astype(BF16)
    context = matmul(permute, context, TN)

    for at, offset in enumerate((1, -1)):
        leaving = jnp.zeros((length, head), F32)
        for r in range(rows):
            leaving = jnp.where(moves(r, offset), context[r * length : (r + 1) * length], leaving)
        ctx_send[at] = leaving.astype(BF16)
    ctx_copies = []
    for at, (slot, target) in enumerate(((rows, right), (rows + 1, left))):
        copy = pltpu.make_async_remote_copy(
            src_ref=ctx_send.at[at],
            dst_ref=context_ref.at[slot],
            send_sem=ctx_send_sem.at[at],
            recv_sem=ctx_recv_sem.at[at],
            device_id={"dp": target},
            device_id_type=MESH,
        )
        copy.start()
        ctx_copies.append(copy)
    for r in range(rows):
        own = jnp.where(moves(r, 0), context[r * length : (r + 1) * length], 0.0)
        context_ref[r] = own.astype(BF16)

    span_own = jnp.concatenate(
        [span_column(r, my_mp * seg, seg) for r in range(rows)], axis=0
    )
    for chunk in range(BACK_CHUNKS):
        summed = part_send[chunk, my_mp].astype(F32)
        for step in range(1, mp_count):
            part_copies[chunk][step - 1].wait_recv()
            summed += part_recv[chunk, step - 1].astype(F32)
        for part in range(2):
            block = jnp.where(
                span_own > 0.5, 0.0, summed[part * seg_total : (part + 1) * seg_total]
            ).astype(BF16)
            columns = pl.ds(chunk * back_width + part * half, half)
            for r in range(rows):
                grad_ref[r, :, columns] = block[r * seg : (r + 1) * seg]

    for copies in part_copies:
        for copy in copies:
            copy.wait_send()
    for copy in ctx_copies:
        copy.wait()


def store_kernel(context_ref, grad_ref, context_out, grad_out, sem):
    copies = [
        pltpu.make_async_copy(context_ref, context_out, sem.at[0]),
        pltpu.make_async_copy(grad_ref, grad_out, sem.at[1]),
    ]
    for copy in copies:
        copy.start()
    for copy in copies:
        copy.wait()


def store(context, grad):
    vmem = pl.BlockSpec(memory_space=pltpu.VMEM)
    hbm = pl.BlockSpec(memory_space=pltpu.HBM)
    return pl.pallas_call(
        store_kernel,
        out_shape=(pltpu.HBM(context.shape, BF16), pltpu.HBM(grad.shape, BF16)),
        in_specs=[vmem, vmem],
        out_specs=(hbm, hbm),
        scratch_shapes=[pltpu.SemaphoreType.DMA((2,))],
        compiler_params=pltpu.CompilerParams(vmem_limit_bytes=1024 * 1024),
    )(context, grad)


def shards(
    inputs,
    denoiser,
    span_mask,
    lengths,
    move_plan,
    mode_table,
    sentinel,
    w_query,
    w_key,
    w_value,
    cotangent,
):
    rows, length, width = inputs.shape
    head = w_query.shape[1]
    dp_count = lax.axis_size("dp")
    mp_count = lax.axis_size("mp")
    seg = length // mp_count
    total = rows * length
    block = (2 * rows * seg, width // BACK_CHUNKS // 2)
    vmem = pl.BlockSpec(memory_space=pltpu.VMEM)
    anywhere = pl.BlockSpec(memory_space=pltpu.HBM)
    dma = pltpu.SemaphoreType.DMA
    context, grad = pl.pallas_call(
        functools.partial(kernel, dp_count, mp_count),
        out_shape=(
            pltpu.VMEM(cotangent.shape, BF16),
            pltpu.VMEM((rows, seg, width), BF16),
        ),
        in_specs=[anywhere] * 11,
        out_specs=(vmem, vmem),
        scratch_shapes=[
            pltpu.SMEM((rows,), jnp.int32),
            pltpu.SMEM((rows,), jnp.int32),
            pltpu.SMEM((rows,), jnp.int32),
            pltpu.VMEM((rows, length), jnp.int32),
            pltpu.VMEM(mode_table.shape, BF16),
            pltpu.VMEM((width // LANES, LANES), BF16),
            pltpu.VMEM((rows, length, width), BF16),
            pltpu.VMEM((rows, length, head), BF16),
            pltpu.VMEM((3, width, head), BF16),
            pltpu.VMEM((total, width), F32),
            pltpu.VMEM((total, width), BF16),
            pltpu.VMEM((2, length, head), BF16),
            pltpu.VMEM((2, length, head), BF16),
            pltpu.VMEM((BACK_CHUNKS, mp_count) + block, BF16),
            pltpu.VMEM((BACK_CHUNKS, mp_count - 1) + block, BF16),
            dma((6,)),
            dma((2,)),
            dma((3, FORWARD_CHUNKS)),
            dma((2,)),
            dma((2,)),
            dma((2,)),
            dma((2,)),
            dma((BACK_CHUNKS, mp_count - 1)),
            dma((BACK_CHUNKS, mp_count - 1)),
        ],
        compiler_params=pltpu.CompilerParams(
            collective_id=0, has_side_effects=True, vmem_limit_bytes=48 * 1024 * 1024
        ),
        cost_estimate=pl.CostEstimate(
            flops=4 * total * width * 3 * head,
            bytes_accessed=2 * 3 * width * head + 4 * total * width,
            transcendentals=total * total,
        ),
    )(
        *[
            pltpu.with_memory_space_constraint(operand, pltpu.HBM)
            for operand in (
                denoiser,
                lengths,
                move_plan,
                span_mask,
                mode_table,
                sentinel.reshape(width // LANES, LANES),
                inputs,
                cotangent,
                w_query,
                w_key,
                w_value,
            )
        ]
    )
    return store(context, grad)


def solution(mesh):
    return jax.shard_map(
        shards,
        mesh=mesh,
        in_specs=(
            P("dp", None, None),
            P("dp"),
            P("dp", None),
            P("dp"),
            P("dp"),
            P(),
            P(),
            P(None, "mp"),
            P(None, "mp"),
            P(None, "mp"),
            P("dp", None, "mp"),
        ),
        out_specs=(P("dp", None, "mp"), P("dp", "mp", None)),
        check_vma=False,
    )
```

```python
import functools
import math

import jax
import jax.numpy as jnp
from jax import lax
from jax.experimental import pallas as pl
from jax.experimental.pallas import tpu as pltpu
from jax.sharding import PartitionSpec as P

MESH = pl.DeviceIdType.MESH
F32 = jnp.float32
BF16 = jnp.bfloat16
NT = (((1,), (1,)), ((), ()))
TN = (((0,), (0,)), ((), ()))
NN = (((1,), (0,)), ((), ()))

FORWARD_CHUNKS = 4
BACK_CHUNKS = 8
NORM_CHUNKS = 4
LANES = 128


def matmul(a, b, dims=NN):
    return lax.dot_general(a, b, dims, preferred_element_type=F32)


def kernel(
    dp_count,
    mp_count,
    denoiser_hbm,
    lengths_hbm,
    move_hbm,
    span_hbm,
    table_hbm,
    sentinel_hbm,
    inputs_hbm,
    cot_hbm,
    wq_hbm,
    wk_hbm,
    wv_hbm,
    context_ref,
    grad_ref,
    denoiser_ref,
    lengths_ref,
    move_ref,
    span_ref,
    table_ref,
    sentinel_ref,
    inputs_ref,
    cot_ref,
    weights,
    normed_ref,
    normed_b_ref,
    cot_recv,
    ctx_send,
    part_send,
    part_recv,
    pair_recv,
    pair_send,
    mate_recv,
    mate_sem,
    small_sem,
    in_sem,
    w_sem,
    cot_send_sem,
    cot_recv_sem,
    ctx_send_sem,
    ctx_recv_sem,
    part_send_sem,
    part_recv_sem,
):
    rows, length, width = inputs_ref.shape
    head = weights.shape[2]
    seg = length // mp_count
    total = rows * length
    seg_total = rows * seg
    mode_count = table_ref.shape[0]
    my_dp = lax.axis_index("dp")
    my_mp = lax.axis_index("mp")
    right = lax.rem(my_dp + 1, dp_count)
    left = lax.rem(my_dp + dp_count - 1, dp_count)

    barrier = pltpu.get_barrier_semaphore()
    for neighbour in (left, right):
        pl.semaphore_signal(barrier, inc=1, device_id={"dp": neighbour}, device_id_type=MESH)
    for step in range(1, mp_count):
        pl.semaphore_signal(
            barrier,
            inc=1,
            device_id={"mp": lax.rem(my_mp + step, mp_count)},
            device_id_type=MESH,
        )

    small_loads = []
    for at, (source, target) in enumerate(
        (
            (denoiser_hbm, denoiser_ref),
            (lengths_hbm, lengths_ref),
            (move_hbm, move_ref),
            (span_hbm, span_ref),
            (table_hbm, table_ref),
            (sentinel_hbm, sentinel_ref),
        )
    ):
        load = pltpu.make_async_copy(source, target, small_sem.at[at])
        load.start()
        small_loads.append(load)
    load_inputs = pltpu.make_async_copy(inputs_hbm, inputs_ref, in_sem.at[0])
    load_inputs.start()
    load_cot = pltpu.make_async_copy(cot_hbm.at[pl.ds(0, rows)], cot_ref, in_sem.at[1])
    load_cot.start()
    depth = width // FORWARD_CHUNKS
    loads = []
    for which, source in enumerate((wq_hbm, wk_hbm, wv_hbm)):
        for chunk in range(FORWARD_CHUNKS):
            piece = pl.ds(chunk * depth, depth)
            load = pltpu.make_async_copy(
                source.at[piece], weights.at[which, piece], w_sem.at[which, chunk]
            )
            load.start()
            loads.append(load)

    for load in small_loads:
        load.wait()

    def split(index):
        row = lax.rem(lax.div(index, seg), rows)
        place = lax.div(index, seg_total) * seg + lax.rem(index, seg)
        return row, place

    def per_row(row, ref):
        value = jnp.zeros_like(row)
        for r in range(rows):
            value = jnp.where(row == r, ref[r], value)
        return value

    col_row, col_place = split(lax.broadcasted_iota(jnp.int32, (total, 1), 0))
    lane_row, lane_place = split(lax.broadcasted_iota(jnp.int32, (1, total), 1))
    natural_lane = lax.broadcasted_iota(jnp.int32, (total, total), 1)
    permute = (natural_lane == col_row * length + col_place).astype(F32).astype(BF16)
    col_len = per_row(col_row, lengths_ref)
    key_ok = (col_row == lane_row) & (lane_place < jnp.maximum(col_len, 1))
    query_ok = col_place < col_len

    def span_column(r, start, count):
        flags = jnp.broadcast_to(span_ref[r : r + 1, :], (count, length))
        place = lax.broadcasted_iota(jnp.int32, (count, length), 0) + start
        lane = lax.broadcasted_iota(jnp.int32, (count, length), 1)
        return jnp.sum(
            jnp.where((place == lane) & (flags == 1), 1.0, 0.0), axis=1, keepdims=True
        )

    span_natural = [span_column(r, 0, length) for r in range(rows)]
    denoiser_col = [jnp.full((1, 1), denoiser_ref[r], jnp.int32) for r in range(rows)]

    load_inputs.wait()
    norm_width = width // NORM_CHUNKS
    squares = jnp.zeros((total, 1), F32)
    for chunk in range(NORM_CHUNKS):
        columns = pl.ds(chunk * norm_width, norm_width)
        lines = norm_width // LANES
        lines_f32 = sentinel_ref[pl.ds(chunk * lines, lines), :].astype(F32)
        sentinel = jnp.concatenate([lines_f32[i : i + 1] for i in range(lines)], axis=1)
        table = table_ref[:, columns].astype(F32)
        pieces = []
        for r in range(rows):
            mode_row = jnp.zeros((1, norm_width), F32)
            for mode in range(mode_count):
                mode_row = jnp.where(denoiser_col[r] == mode, table[mode : mode + 1], mode_row)
            plain = inputs_ref[r, :, columns].astype(F32) + mode_row
            pieces.append(jnp.where(span_natural[r] > 0.5, sentinel, plain).astype(BF16))
        shaped = matmul(permute, jnp.concatenate(pieces, axis=0))
        normed_ref[:, columns] = shaped
        squares += jnp.sum(shaped * shaped, axis=1, keepdims=True)
    inv_rms = lax.rsqrt(squares * (1.0 / width) + 1e-06)
    for chunk in range(NORM_CHUNKS):
        columns = pl.ds(chunk * norm_width, norm_width)
        normed = normed_ref[:, columns] * inv_rms
        normed_ref[:, columns] = normed
        normed_b_ref[:, columns] = normed.astype(BF16)

    pl.semaphore_wait(barrier, 2 + mp_count - 1)
    cot_copies = []
    for at, (slot, home) in enumerate(((rows, left), (rows + 1, right))):
        copy = pltpu.make_async_remote_copy(
            src_ref=cot_hbm.at[slot],
            dst_ref=cot_recv.at[at],
            send_sem=cot_send_sem.at[at],
            recv_sem=cot_recv_sem.at[at],
            device_id={"dp": home},
            device_id_type=MESH,
        )
        copy.start()
        cot_copies.append(copy)

    def project(which, chunk):
        piece = pl.ds(chunk * depth, depth)
        return matmul(normed_b_ref[:, piece], weights[which, piece, :])

    query_f32 = jnp.zeros((total, head), F32)
    key_f32 = jnp.zeros((total, head), F32)
    for chunk in range(FORWARD_CHUNKS):
        loads[chunk].wait()
        query_f32 += project(0, chunk)
    for chunk in range(FORWARD_CHUNKS):
        loads[FORWARD_CHUNKS + chunk].wait()
        key_f32 += project(1, chunk)
    for chunk in range(FORWARD_CHUNKS):
        loads[2 * FORWARD_CHUNKS + chunk].wait()
    load_cot.wait()
    for copy in cot_copies:
        copy.wait()

    query = query_f32.astype(BF16)
    key = key_f32.astype(BF16)
    factor = 1.0 / math.sqrt(head)
    scores = jnp.where(key_ok, matmul(query, key, NT) * factor, -jnp.inf)
    value_f32 = project(2, 0)
    for chunk in range(1, FORWARD_CHUNKS):
        value_f32 += project(2, chunk)
    exp_scores = jnp.exp(scores - jnp.max(scores, axis=1, keepdims=True))
    soft = exp_scores / jnp.sum(exp_scores, axis=1, keepdims=True)
    soft_b = soft.astype(BF16)
    value = value_f32.astype(BF16)
    projected = (query_f32, key_f32, value_f32)

    def moves(r, offset):
        return jnp.full((1, 1), move_ref[r], jnp.int32) == offset

    from_right = cot_recv[0].astype(F32)
    from_left = cot_recv[1].astype(F32)
    pieces = []
    for r in range(rows):
        moved = jnp.where(moves(r, 1), from_right, from_left)
        pieces.append(jnp.where(moves(r, 0), cot_ref[r].astype(F32), moved).astype(BF16))
    grad_out = matmul(permute, jnp.concatenate(pieces, axis=0))
    grad_out = jnp.where(query_ok, grad_out, 0.0).astype(BF16)

    grad_value = matmul(soft_b, grad_out, TN).astype(BF16)
    grad_soft = matmul(grad_out, value, NT)
    row_inner = jnp.sum(soft * grad_soft, axis=1, keepdims=True)
    grad_scores = (soft * (grad_soft - row_inner) * factor).astype(BF16)
    grad_query = matmul(grad_scores, key).astype(BF16)
    grad_key = matmul(grad_scores, query, TN).astype(BF16)
    gradients = (grad_query, grad_key, grad_value)
    inner = jnp.zeros((total, 1), F32)
    for gradient, result in zip(gradients, projected):
        inner += jnp.sum(gradient.astype(F32) * result, axis=1, keepdims=True)
    inner = inner * (1.0 / width)

    back_width = width // BACK_CHUNKS
    half = back_width // 2
    paired = mp_count == 4
    mate = my_mp + 1 - 2 * lax.rem(my_mp, 2)
    other = 2 - 2 * lax.div(my_mp, 2)
    outer = (my_mp == 0) | (my_mp == mp_count - 1)

    def remote(source, target, send_sem, recv_sem, peer):
        return pltpu.make_async_remote_copy(
            src_ref=source,
            dst_ref=target,
            send_sem=send_sem,
            recv_sem=recv_sem,
            device_id={"mp": peer},
            device_id_type=MESH,
        )

    def back(chunk):
        piece = pl.ds(chunk * back_width, back_width)
        head_grad = matmul(gradients[0], weights[0, piece, :], NT)
        head_grad += matmul(gradients[1], weights[1, piece, :], NT)
        head_grad += matmul(gradients[2], weights[2, piece, :], NT)
        return head_grad

    def to_mate(chunk):
        return remote(
            part_send.at[chunk, pl.ds(other, 2)],
            pair_recv.at[chunk],
            part_send_sem.at[chunk, 0],
            part_recv_sem.at[chunk, 0],
            mate,
        )

    def from_inner(chunk, j):
        return remote(
            pair_send.at[chunk, j],
            part_recv.at[chunk, 0],
            part_send_sem.at[chunk, 1 + j],
            part_recv_sem.at[chunk, 1],
            other + j,
        )

    def direct(chunk, step):
        peer = lax.rem(my_mp + step, mp_count)
        return remote(
            part_send.at[chunk, peer],
            part_recv.at[chunk, step - 1],
            part_send_sem.at[chunk, step - 1],
            part_recv_sem.at[chunk, step - 1],
            peer,
        )

    head_grad = back(0)
    for chunk in range(BACK_CHUNKS):
        piece = pl.ds(chunk * back_width, back_width)
        following = back(chunk + 1) if chunk + 1 < BACK_CHUNKS else None
        head_part = (head_grad - normed_ref[:, piece] * inner) * inv_rms
        for s in range(mp_count):
            block = head_part[s * seg_total : (s + 1) * seg_total]
            stacked = jnp.concatenate([block[:, :half], block[:, half:]], axis=0)
            part_send[chunk, s] = stacked.astype(BF16)
        if paired:

            @pl.when(outer)
            def _():
                to_mate(chunk).start()

        else:
            for step in range(1, mp_count):
                direct(chunk, step).start()
        head_grad = following

    if paired:
        mate_copy = remote(
            part_send.at[:, mate], mate_recv, mate_sem.at[0], mate_sem.at[1], mate
        )
        mate_copy.start()

    context = jnp.where(query_ok, matmul(soft_b, value), 0.0).astype(BF16)
    context = matmul(permute, context, TN)

    for at, offset in enumerate((1, -1)):
        leaving = jnp.zeros((length, head), F32)
        for r in range(rows):
            leaving = jnp.where(moves(r, offset), context[r * length : (r + 1) * length], leaving)
        ctx_send[at] = leaving.astype(BF16)
    ctx_copies = []
    for at, (slot, target) in enumerate(((rows, right), (rows + 1, left))):
        copy = pltpu.make_async_remote_copy(
            src_ref=ctx_send.at[at],
            dst_ref=context_ref.at[slot],
            send_sem=ctx_send_sem.at[at],
            recv_sem=ctx_recv_sem.at[at],
            device_id={"dp": target},
            device_id_type=MESH,
        )
        copy.start()
        ctx_copies.append(copy)
    for r in range(rows):
        own = jnp.where(moves(r, 0), context[r * length : (r + 1) * length], 0.0)
        context_ref[r] = own.astype(BF16)

    if paired:

        @pl.when(jnp.logical_not(outer))
        def _():
            for chunk in range(BACK_CHUNKS):
                to_mate(chunk).wait_recv()
                for j in range(2):
                    partial = part_send[chunk, other + j].astype(F32)
                    partial += pair_recv[chunk, j].astype(F32)
                    pair_send[chunk, j] = partial.astype(BF16)
                    from_inner(chunk, j).start()

        mate_copy.wait_recv()

    span_own = jnp.concatenate(
        [span_column(r, my_mp * seg, seg) for r in range(rows)], axis=0
    )
    for chunk in range(BACK_CHUNKS):
        summed = part_send[chunk, my_mp].astype(F32)
        if paired:
            summed += mate_recv[chunk].astype(F32)
            from_inner(chunk, 0).wait_recv()
            summed += part_recv[chunk, 0].astype(F32)
        else:
            for step in range(1, mp_count):
                direct(chunk, step).wait_recv()
                summed += part_recv[chunk, step - 1].astype(F32)
        for part in range(2):
            block = jnp.where(
                span_own > 0.5, 0.0, summed[part * seg_total : (part + 1) * seg_total]
            ).astype(BF16)
            columns = pl.ds(chunk * back_width + part * half, half)
            for r in range(rows):
                grad_ref[r, :, columns] = block[r * seg : (r + 1) * seg]

    if paired:
        mate_copy.wait_send()

        @pl.when(outer)
        def _():
            for chunk in range(BACK_CHUNKS):
                to_mate(chunk).wait_send()

        @pl.when(jnp.logical_not(outer))
        def _():
            for chunk in range(BACK_CHUNKS):
                for j in range(2):
                    from_inner(chunk, j).wait_send()

    else:
        for chunk in range(BACK_CHUNKS):
            for step in range(1, mp_count):
                direct(chunk, step).wait_send()
    for copy in ctx_copies:
        copy.wait()


def store_kernel(context_ref, grad_ref, context_out, grad_out, sem):
    copies = [
        pltpu.make_async_copy(context_ref, context_out, sem.at[0]),
        pltpu.make_async_copy(grad_ref, grad_out, sem.at[1]),
    ]
    for copy in copies:
        copy.start()
    for copy in copies:
        copy.wait()


def store(context, grad):
    vmem = pl.BlockSpec(memory_space=pltpu.VMEM)
    hbm = pl.BlockSpec(memory_space=pltpu.HBM)
    return pl.pallas_call(
        store_kernel,
        out_shape=(pltpu.HBM(context.shape, BF16), pltpu.HBM(grad.shape, BF16)),
        in_specs=[vmem, vmem],
        out_specs=(hbm, hbm),
        scratch_shapes=[pltpu.SemaphoreType.DMA((2,))],
        compiler_params=pltpu.CompilerParams(vmem_limit_bytes=1024 * 1024),
    )(context, grad)


def shards(
    inputs,
    denoiser,
    span_mask,
    lengths,
    move_plan,
    mode_table,
    sentinel,
    w_query,
    w_key,
    w_value,
    cotangent,
):
    rows, length, width = inputs.shape
    head = w_query.shape[1]
    dp_count = lax.axis_size("dp")
    mp_count = lax.axis_size("mp")
    seg = length // mp_count
    total = rows * length
    block = (2 * rows * seg, width // BACK_CHUNKS // 2)
    vmem = pl.BlockSpec(memory_space=pltpu.VMEM)
    anywhere = pl.BlockSpec(memory_space=pltpu.HBM)
    dma = pltpu.SemaphoreType.DMA
    context, grad = pl.pallas_call(
        functools.partial(kernel, dp_count, mp_count),
        out_shape=(
            pltpu.VMEM(cotangent.shape, BF16),
            pltpu.VMEM((rows, seg, width), BF16),
        ),
        in_specs=[anywhere] * 11,
        out_specs=(vmem, vmem),
        scratch_shapes=[
            pltpu.SMEM((rows,), jnp.int32),
            pltpu.SMEM((rows,), jnp.int32),
            pltpu.SMEM((rows,), jnp.int32),
            pltpu.VMEM((rows, length), jnp.int32),
            pltpu.VMEM(mode_table.shape, BF16),
            pltpu.VMEM((width // LANES, LANES), BF16),
            pltpu.VMEM((rows, length, width), BF16),
            pltpu.VMEM((rows, length, head), BF16),
            pltpu.VMEM((3, width, head), BF16),
            pltpu.VMEM((total, width), F32),
            pltpu.VMEM((total, width), BF16),
            pltpu.VMEM((2, length, head), BF16),
            pltpu.VMEM((2, length, head), BF16),
            pltpu.VMEM((BACK_CHUNKS, mp_count) + block, BF16),
            pltpu.VMEM((BACK_CHUNKS, mp_count - 1) + block, BF16),
            pltpu.VMEM((BACK_CHUNKS, 2) + block, BF16),
            pltpu.VMEM((BACK_CHUNKS, 2) + block, BF16),
            pltpu.VMEM((BACK_CHUNKS,) + block, BF16),
            dma((2,)),
            dma((6,)),
            dma((2,)),
            dma((3, FORWARD_CHUNKS)),
            dma((2,)),
            dma((2,)),
            dma((2,)),
            dma((2,)),
            dma((BACK_CHUNKS, mp_count - 1)),
            dma((BACK_CHUNKS, mp_count - 1)),
        ],
        compiler_params=pltpu.CompilerParams(
            collective_id=0, has_side_effects=True, vmem_limit_bytes=48 * 1024 * 1024
        ),
        cost_estimate=pl.CostEstimate(
            flops=4 * total * width * 3 * head,
            bytes_accessed=2 * 3 * width * head + 4 * total * width,
            transcendentals=total * total,
        ),
    )(
        *[
            pltpu.with_memory_space_constraint(operand, pltpu.HBM)
            for operand in (
                denoiser,
                lengths,
                move_plan,
                span_mask,
                mode_table,
                sentinel.reshape(width // LANES, LANES),
                inputs,
                cotangent,
                w_query,
                w_key,
                w_value,
            )
        ]
    )
    return store(context, grad)


def solution(mesh):
    return jax.shard_map(
        shards,
        mesh=mesh,
        in_specs=(
            P("dp", None, None),
            P("dp"),
            P("dp", None),
            P("dp"),
            P("dp"),
            P(),
            P(),
            P(None, "mp"),
            P(None, "mp"),
            P(None, "mp"),
            P("dp", None, "mp"),
        ),
        out_specs=(P("dp", None, "mp"), P("dp", "mp", None)),
        check_vma=False,
    )
```

```python
import functools
import math

import jax
import jax.numpy as jnp
from jax import lax
from jax.experimental import pallas as pl
from jax.experimental.pallas import tpu as pltpu
from jax.sharding import PartitionSpec as P

MESH = pl.DeviceIdType.MESH
F32 = jnp.float32
BF16 = jnp.bfloat16
NT = (((1,), (1,)), ((), ()))
TN = (((0,), (0,)), ((), ()))
NN = (((1,), (0,)), ((), ()))

FORWARD_CHUNKS = 2
BACK_CHUNKS = 4
NORM_CHUNKS = 4
LANES = 128


def matmul(a, b, dims=NN):
    return lax.dot_general(a, b, dims, preferred_element_type=F32)


def kernel(
    dp_count,
    mp_count,
    denoiser_hbm,
    lengths_hbm,
    move_hbm,
    span_hbm,
    table_hbm,
    sentinel_hbm,
    inputs_hbm,
    cot_hbm,
    wq_hbm,
    wk_hbm,
    wv_hbm,
    context_ref,
    grad_ref,
    denoiser_ref,
    lengths_ref,
    move_ref,
    span_ref,
    table_ref,
    sentinel_ref,
    inputs_ref,
    cot_ref,
    weights,
    normed_ref,
    normed_b_ref,
    cot_recv,
    ctx_send,
    part_send,
    part_recv,
    small_sem,
    in_sem,
    w_sem,
    cot_send_sem,
    cot_recv_sem,
    ctx_send_sem,
    ctx_recv_sem,
    part_send_sem,
    part_recv_sem,
):
    rows, length, width = inputs_ref.shape
    head = weights.shape[2]
    seg = length // mp_count
    total = rows * length
    seg_total = rows * seg
    mode_count = table_ref.shape[0]
    my_dp = lax.axis_index("dp")
    my_mp = lax.axis_index("mp")
    right = lax.rem(my_dp + 1, dp_count)
    left = lax.rem(my_dp + dp_count - 1, dp_count)

    barrier = pltpu.get_barrier_semaphore()
    for neighbour in (left, right):
        pl.semaphore_signal(barrier, inc=1, device_id={"dp": neighbour}, device_id_type=MESH)
    for step in range(1, mp_count):
        pl.semaphore_signal(
            barrier,
            inc=1,
            device_id={"mp": lax.rem(my_mp + step, mp_count)},
            device_id_type=MESH,
        )

    small_loads = []
    for at, (source, target) in enumerate(
        (
            (denoiser_hbm, denoiser_ref),
            (lengths_hbm, lengths_ref),
            (move_hbm, move_ref),
            (span_hbm, span_ref),
            (table_hbm, table_ref),
            (sentinel_hbm, sentinel_ref),
        )
    ):
        load = pltpu.make_async_copy(source, target, small_sem.at[at])
        load.start()
        small_loads.append(load)
    load_inputs = pltpu.make_async_copy(inputs_hbm, inputs_ref, in_sem.at[0])
    load_inputs.start()
    load_cot = pltpu.make_async_copy(cot_hbm.at[pl.ds(0, rows)], cot_ref, in_sem.at[1])
    load_cot.start()
    depth = width // FORWARD_CHUNKS
    loads = []
    for which, source in enumerate((wq_hbm, wk_hbm, wv_hbm)):
        for chunk in range(FORWARD_CHUNKS):
            piece = pl.ds(chunk * depth, depth)
            load = pltpu.make_async_copy(
                source.at[piece], weights.at[which, piece], w_sem.at[which, chunk]
            )
            load.start()
            loads.append(load)

    for load in small_loads:
        load.wait()

    def split(index):
        row = lax.rem(lax.div(index, seg), rows)
        place = lax.div(index, seg_total) * seg + lax.rem(index, seg)
        return row, place

    def per_row(row, ref):
        value = jnp.zeros_like(row)
        for r in range(rows):
            value = jnp.where(row == r, ref[r], value)
        return value

    col_row, col_place = split(lax.broadcasted_iota(jnp.int32, (total, 1), 0))
    lane_row, _ = split(lax.broadcasted_iota(jnp.int32, (1, total), 1))
    natural_lane = lax.broadcasted_iota(jnp.int32, (total, total), 1)
    permute = (natural_lane == col_row * length + col_place).astype(F32).astype(BF16)
    col_len = per_row(col_row, lengths_ref)
    key_ok = (col_row == lane_row) & (col_place < jnp.maximum(col_len, 1))
    query_ok = col_place < col_len

    def span_column(r, start, count):
        flags = jnp.broadcast_to(span_ref[r : r + 1, :], (count, length))
        place = lax.broadcasted_iota(jnp.int32, (count, length), 0) + start
        lane = lax.broadcasted_iota(jnp.int32, (count, length), 1)
        return jnp.sum(
            jnp.where((place == lane) & (flags == 1), 1.0, 0.0), axis=1, keepdims=True
        )

    span_natural = [span_column(r, 0, length) for r in range(rows)]
    denoiser_col = [jnp.full((1, 1), denoiser_ref[r], jnp.int32) for r in range(rows)]

    load_inputs.wait()
    norm_width = width // NORM_CHUNKS
    squares = jnp.zeros((total, 1), F32)
    for chunk in range(NORM_CHUNKS):
        columns = pl.ds(chunk * norm_width, norm_width)
        lines = norm_width // LANES
        lines_f32 = sentinel_ref[pl.ds(chunk * lines, lines), :].astype(F32)
        sentinel = jnp.concatenate([lines_f32[i : i + 1] for i in range(lines)], axis=1)
        table = table_ref[:, columns].astype(F32)
        pieces = []
        for r in range(rows):
            mode_row = jnp.zeros((1, norm_width), F32)
            for mode in range(mode_count):
                mode_row = jnp.where(denoiser_col[r] == mode, table[mode : mode + 1], mode_row)
            plain = inputs_ref[r, :, columns].astype(F32) + mode_row
            pieces.append(jnp.where(span_natural[r] > 0.5, sentinel, plain).astype(BF16))
        shaped = matmul(permute, jnp.concatenate(pieces, axis=0))
        normed_ref[:, columns] = shaped
        squares += jnp.sum(shaped * shaped, axis=1, keepdims=True)
    inv_rms = lax.rsqrt(squares * (1.0 / width) + 1e-06)
    for chunk in range(NORM_CHUNKS):
        columns = pl.ds(chunk * norm_width, norm_width)
        normed = normed_ref[:, columns] * inv_rms
        normed_ref[:, columns] = normed
        normed_b_ref[:, columns] = normed.astype(BF16)

    pl.semaphore_wait(barrier, 2 + mp_count - 1)
    cot_copies = []
    for at, (slot, home) in enumerate(((rows, left), (rows + 1, right))):
        copy = pltpu.make_async_remote_copy(
            src_ref=cot_hbm.at[slot],
            dst_ref=cot_recv.at[at],
            send_sem=cot_send_sem.at[at],
            recv_sem=cot_recv_sem.at[at],
            device_id={"dp": home},
            device_id_type=MESH,
        )
        copy.start()
        cot_copies.append(copy)

    def project(which, chunk):
        piece = pl.ds(chunk * depth, depth)
        return matmul(normed_b_ref[:, piece], weights[which, piece, :])

    query_f32 = jnp.zeros((total, head), F32)
    key_f32 = jnp.zeros((total, head), F32)
    for chunk in range(FORWARD_CHUNKS):
        loads[chunk].wait()
        query_f32 += project(0, chunk)
    for chunk in range(FORWARD_CHUNKS):
        loads[FORWARD_CHUNKS + chunk].wait()
        key_f32 += project(1, chunk)
    for chunk in range(FORWARD_CHUNKS):
        loads[2 * FORWARD_CHUNKS + chunk].wait()
    load_cot.wait()
    for copy in cot_copies:
        copy.wait()

    query = query_f32.astype(BF16)
    key = key_f32.astype(BF16)
    factor = 1.0 / math.sqrt(head)
    scores = jnp.where(key_ok, matmul(key, query, NT) * factor, -jnp.inf)
    value_f32 = project(2, 0)
    for chunk in range(1, FORWARD_CHUNKS):
        value_f32 += project(2, chunk)
    exp_scores = jnp.exp(scores - jnp.max(scores, axis=0, keepdims=True))
    soft = exp_scores / jnp.sum(exp_scores, axis=0, keepdims=True)
    soft_b = soft.astype(BF16)
    value = value_f32.astype(BF16)
    projected = (query_f32, key_f32, value_f32)

    def moves(r, offset):
        return jnp.full((1, 1), move_ref[r], jnp.int32) == offset

    from_right = cot_recv[0].astype(F32)
    from_left = cot_recv[1].astype(F32)
    pieces = []
    for r in range(rows):
        moved = jnp.where(moves(r, 1), from_right, from_left)
        pieces.append(jnp.where(moves(r, 0), cot_ref[r].astype(F32), moved).astype(BF16))
    grad_out = matmul(permute, jnp.concatenate(pieces, axis=0))
    grad_out = jnp.where(query_ok, grad_out, 0.0).astype(BF16)

    grad_value = matmul(soft_b, grad_out).astype(BF16)
    grad_soft = matmul(value, grad_out, NT)
    row_inner = jnp.sum(soft * grad_soft, axis=0, keepdims=True)
    grad_scores = (soft * (grad_soft - row_inner) * factor).astype(BF16)
    grad_query = matmul(grad_scores, key, TN).astype(BF16)
    grad_key = matmul(grad_scores, query).astype(BF16)
    gradients = (grad_query, grad_key, grad_value)
    inner = jnp.zeros((total, 1), F32)
    for gradient, result in zip(gradients, projected):
        inner += jnp.sum(gradient.astype(F32) * result, axis=1, keepdims=True)
    inner = inner * (1.0 / width)

    back_width = width // BACK_CHUNKS
    half = back_width // 2

    def remote(source, target, send_sem, recv_sem, peer):
        return pltpu.make_async_remote_copy(
            src_ref=source,
            dst_ref=target,
            send_sem=send_sem,
            recv_sem=recv_sem,
            device_id={"mp": peer},
            device_id_type=MESH,
        )

    def back(chunk):
        piece = pl.ds(chunk * back_width, back_width)
        head_grad = matmul(gradients[0], weights[0, piece, :], NT)
        head_grad += matmul(gradients[1], weights[1, piece, :], NT)
        head_grad += matmul(gradients[2], weights[2, piece, :], NT)
        return head_grad

    def direct(chunk, step):
        peer = lax.rem(my_mp + step, mp_count)
        return remote(
            part_send.at[chunk, peer],
            part_recv.at[chunk, step - 1],
            part_send_sem.at[chunk, step - 1],
            part_recv_sem.at[chunk, step - 1],
            peer,
        )

    head_grad = back(0)
    for chunk in range(BACK_CHUNKS):
        piece = pl.ds(chunk * back_width, back_width)
        following = back(chunk + 1) if chunk + 1 < BACK_CHUNKS else None
        head_part = (head_grad - normed_ref[:, piece] * inner) * inv_rms
        for s in range(mp_count):
            block = head_part[s * seg_total : (s + 1) * seg_total]
            stacked = jnp.concatenate([block[:, :half], block[:, half:]], axis=0)
            part_send[chunk, s] = stacked.astype(BF16)
        for step in range(1, mp_count):
            direct(chunk, step).start()
        head_grad = following

    context = jnp.where(query_ok, matmul(soft_b, value, TN), 0.0).astype(BF16)
    context = matmul(permute, context, TN)

    for at, offset in enumerate((1, -1)):
        leaving = jnp.zeros((length, head), F32)
        for r in range(rows):
            leaving = jnp.where(moves(r, offset), context[r * length : (r + 1) * length], leaving)
        ctx_send[at] = leaving.astype(BF16)
    ctx_copies = []
    for at, (slot, target) in enumerate(((rows, right), (rows + 1, left))):
        copy = pltpu.make_async_remote_copy(
            src_ref=ctx_send.at[at],
            dst_ref=context_ref.at[slot],
            send_sem=ctx_send_sem.at[at],
            recv_sem=ctx_recv_sem.at[at],
            device_id={"dp": target},
            device_id_type=MESH,
        )
        copy.start()
        ctx_copies.append(copy)
    for r in range(rows):
        own = jnp.where(moves(r, 0), context[r * length : (r + 1) * length], 0.0)
        context_ref[r] = own.astype(BF16)

    span_own = jnp.concatenate(
        [span_column(r, my_mp * seg, seg) for r in range(rows)], axis=0
    )
    for chunk in range(BACK_CHUNKS):
        summed = part_send[chunk, my_mp].astype(F32)
        for step in range(1, mp_count):
            direct(chunk, step).wait_recv()
            summed += part_recv[chunk, step - 1].astype(F32)
        for part in range(2):
            block = jnp.where(
                span_own > 0.5, 0.0, summed[part * seg_total : (part + 1) * seg_total]
            ).astype(BF16)
            columns = pl.ds(chunk * back_width + part * half, half)
            for r in range(rows):
                grad_ref[r, :, columns] = block[r * seg : (r + 1) * seg]

    for chunk in range(BACK_CHUNKS):
        for step in range(1, mp_count):
            direct(chunk, step).wait_send()
    for copy in ctx_copies:
        copy.wait()


def store_kernel(context_ref, grad_ref, context_out, grad_out, sem):
    copies = [
        pltpu.make_async_copy(context_ref, context_out, sem.at[0]),
        pltpu.make_async_copy(grad_ref, grad_out, sem.at[1]),
    ]
    for copy in copies:
        copy.start()
    for copy in copies:
        copy.wait()


def store(context, grad):
    vmem = pl.BlockSpec(memory_space=pltpu.VMEM)
    hbm = pl.BlockSpec(memory_space=pltpu.HBM)
    return pl.pallas_call(
        store_kernel,
        out_shape=(pltpu.HBM(context.shape, BF16), pltpu.HBM(grad.shape, BF16)),
        in_specs=[vmem, vmem],
        out_specs=(hbm, hbm),
        scratch_shapes=[pltpu.SemaphoreType.DMA((2,))],
        compiler_params=pltpu.CompilerParams(vmem_limit_bytes=1024 * 1024),
    )(context, grad)


def shards(
    inputs,
    denoiser,
    span_mask,
    lengths,
    move_plan,
    mode_table,
    sentinel,
    w_query,
    w_key,
    w_value,
    cotangent,
):
    rows, length, width = inputs.shape
    head = w_query.shape[1]
    dp_count = lax.axis_size("dp")
    mp_count = lax.axis_size("mp")
    seg = length // mp_count
    total = rows * length
    block = (2 * rows * seg, width // BACK_CHUNKS // 2)
    vmem = pl.BlockSpec(memory_space=pltpu.VMEM)
    anywhere = pl.BlockSpec(memory_space=pltpu.HBM)
    dma = pltpu.SemaphoreType.DMA
    context, grad = pl.pallas_call(
        functools.partial(kernel, dp_count, mp_count),
        out_shape=(
            pltpu.VMEM(cotangent.shape, BF16),
            pltpu.VMEM((rows, seg, width), BF16),
        ),
        in_specs=[anywhere] * 11,
        out_specs=(vmem, vmem),
        scratch_shapes=[
            pltpu.SMEM((rows,), jnp.int32),
            pltpu.SMEM((rows,), jnp.int32),
            pltpu.SMEM((rows,), jnp.int32),
            pltpu.VMEM((rows, length), jnp.int32),
            pltpu.VMEM(mode_table.shape, BF16),
            pltpu.VMEM((width // LANES, LANES), BF16),
            pltpu.VMEM((rows, length, width), BF16),
            pltpu.VMEM((rows, length, head), BF16),
            pltpu.VMEM((3, width, head), BF16),
            pltpu.VMEM((total, width), F32),
            pltpu.VMEM((total, width), BF16),
            pltpu.VMEM((2, length, head), BF16),
            pltpu.VMEM((2, length, head), BF16),
            pltpu.VMEM((BACK_CHUNKS, mp_count) + block, BF16),
            pltpu.VMEM((BACK_CHUNKS, mp_count - 1) + block, BF16),
            dma((6,)),
            dma((2,)),
            dma((3, FORWARD_CHUNKS)),
            dma((2,)),
            dma((2,)),
            dma((2,)),
            dma((2,)),
            dma((BACK_CHUNKS, mp_count - 1)),
            dma((BACK_CHUNKS, mp_count - 1)),
        ],
        compiler_params=pltpu.CompilerParams(
            collective_id=0, has_side_effects=True, vmem_limit_bytes=48 * 1024 * 1024
        ),
        cost_estimate=pl.CostEstimate(
            flops=4 * total * width * 3 * head,
            bytes_accessed=2 * 3 * width * head + 4 * total * width,
            transcendentals=total * total,
        ),
    )(
        *[
            pltpu.with_memory_space_constraint(operand, pltpu.HBM)
            for operand in (
                denoiser,
                lengths,
                move_plan,
                span_mask,
                mode_table,
                sentinel.reshape(width // LANES, LANES),
                inputs,
                cotangent,
                w_query,
                w_key,
                w_value,
            )
        ]
    )
    return store(context, grad)


def solution(mesh):
    return jax.shard_map(
        shards,
        mesh=mesh,
        in_specs=(
            P("dp", None, None),
            P("dp"),
            P("dp", None),
            P("dp"),
            P("dp"),
            P(),
            P(),
            P(None, "mp"),
            P(None, "mp"),
            P(None, "mp"),
            P("dp", None, "mp"),
        ),
        out_specs=(P("dp", None, "mp"), P("dp", "mp", None)),
        check_vma=False,
    )
```

```python
import functools
import math

import jax
import jax.numpy as jnp
from jax import lax
from jax.experimental import pallas as pl
from jax.experimental.pallas import tpu as pltpu
from jax.sharding import PartitionSpec as P

MESH = pl.DeviceIdType.MESH
F32 = jnp.float32
BF16 = jnp.bfloat16
NT = (((1,), (1,)), ((), ()))
TN = (((0,), (0,)), ((), ()))
NN = (((1,), (0,)), ((), ()))

FORWARD_CHUNKS = 4
BACK_CHUNKS = 4
NORM_CHUNKS = 4
LANES = 128


def matmul(a, b, dims=NN):
    return lax.dot_general(a, b, dims, preferred_element_type=F32)


def kernel(
    dp_count,
    mp_count,
    denoiser_hbm,
    lengths_hbm,
    move_hbm,
    span_hbm,
    table_hbm,
    sentinel_hbm,
    inputs_hbm,
    cot_hbm,
    wq_hbm,
    wk_hbm,
    wv_hbm,
    context_ref,
    grad_ref,
    denoiser_ref,
    lengths_ref,
    move_ref,
    span_ref,
    table_ref,
    sentinel_ref,
    inputs_ref,
    cot_ref,
    weights,
    sentinel_row,
    normed_ref,
    normed_b_ref,
    projected_ref,
    cot_recv,
    ctx_send,
    part_send,
    part_recv,
    small_sem,
    in_sem,
    w_sem,
    cot_send_sem,
    cot_recv_sem,
    ctx_send_sem,
    ctx_recv_sem,
    part_send_sem,
    part_recv_sem,
):
    rows, length, width = inputs_ref.shape
    head = weights.shape[2]
    seg = length // mp_count
    total = rows * length
    seg_total = rows * seg
    mode_count = table_ref.shape[0]
    my_dp = lax.axis_index("dp")
    my_mp = lax.axis_index("mp")
    right = lax.rem(my_dp + 1, dp_count)
    left = lax.rem(my_dp + dp_count - 1, dp_count)

    barrier = pltpu.get_barrier_semaphore()
    for neighbour in (left, right):
        pl.semaphore_signal(barrier, inc=1, device_id={"dp": neighbour}, device_id_type=MESH)
    for step in range(1, mp_count):
        pl.semaphore_signal(
            barrier,
            inc=1,
            device_id={"mp": lax.rem(my_mp + step, mp_count)},
            device_id_type=MESH,
        )

    small_loads = []
    for at, (source, target) in enumerate(
        (
            (denoiser_hbm, denoiser_ref),
            (lengths_hbm, lengths_ref),
            (move_hbm, move_ref),
            (span_hbm, span_ref),
            (table_hbm, table_ref),
            (sentinel_hbm, sentinel_ref),
        )
    ):
        load = pltpu.make_async_copy(source, target, small_sem.at[at])
        load.start()
        small_loads.append(load)
    load_inputs = pltpu.make_async_copy(inputs_hbm, inputs_ref, in_sem.at[0])
    load_inputs.start()
    load_cot = pltpu.make_async_copy(cot_hbm.at[pl.ds(0, rows)], cot_ref, in_sem.at[1])
    load_cot.start()
    depth = width // FORWARD_CHUNKS
    def load_weights(chunk):
        piece = pl.ds(pl.multiple_of(chunk * depth, depth), depth)
        return [
            pltpu.make_async_copy(
                source.at[piece], weights.at[which, piece], w_sem.at[which, chunk]
            )
            for which, source in enumerate((wq_hbm, wk_hbm, wv_hbm))
        ]

    for chunk in range(FORWARD_CHUNKS):
        for load in load_weights(chunk):
            load.start()

    for load in small_loads:
        load.wait()

    def split(index):
        row = lax.rem(lax.div(index, seg), rows)
        place = lax.div(index, seg_total) * seg + lax.rem(index, seg)
        return row, place

    def per_row(row, ref):
        value = jnp.zeros_like(row)
        for r in range(rows):
            value = jnp.where(row == r, ref[r], value)
        return value

    col_row, col_place = split(lax.broadcasted_iota(jnp.int32, (total, 1), 0))
    lane_row, _ = split(lax.broadcasted_iota(jnp.int32, (1, total), 1))
    natural_lane = lax.broadcasted_iota(jnp.int32, (total, total), 1)
    permute = (natural_lane == col_row * length + col_place).astype(F32).astype(BF16)
    col_len = per_row(col_row, lengths_ref)
    key_ok = (col_row == lane_row) & (col_place < jnp.maximum(col_len, 1))
    query_ok = col_place < col_len

    def span_column(r, start, count):
        flags = jnp.broadcast_to(span_ref[r : r + 1, :], (count, length))
        place = lax.broadcasted_iota(jnp.int32, (count, length), 0) + start
        lane = lax.broadcasted_iota(jnp.int32, (count, length), 1)
        return jnp.sum(
            jnp.where((place == lane) & (flags == 1), 1.0, 0.0), axis=1, keepdims=True
        )

    span_natural = [span_column(r, 0, length) for r in range(rows)]
    denoiser_col = [jnp.full((1, 1), denoiser_ref[r], jnp.int32) for r in range(rows)]

    load_inputs.wait()
    lines = sentinel_ref[...].astype(F32)
    for line in range(width // LANES):
        sentinel_row[:, line * LANES : (line + 1) * LANES] = lines[line : line + 1]
    norm_width = width // NORM_CHUNKS

    def shape_chunk(chunk, squares):
        columns = pl.ds(pl.multiple_of(chunk * norm_width, norm_width), norm_width)
        sentinel = sentinel_row[:, columns]
        table = table_ref[:, columns].astype(F32)
        pieces = []
        for r in range(rows):
            mode_row = jnp.zeros((1, norm_width), F32)
            for mode in range(mode_count):
                mode_row = jnp.where(denoiser_col[r] == mode, table[mode : mode + 1], mode_row)
            plain = inputs_ref[r, :, columns].astype(F32) + mode_row
            pieces.append(jnp.where(span_natural[r] > 0.5, sentinel, plain).astype(BF16))
        shaped = matmul(permute, jnp.concatenate(pieces, axis=0))
        normed_ref[:, columns] = shaped
        return squares + jnp.sum(shaped * shaped, axis=1, keepdims=True)

    squares = lax.fori_loop(0, NORM_CHUNKS, shape_chunk, jnp.zeros((total, 1), F32))
    inv_rms = lax.rsqrt(squares * (1.0 / width) + 1e-06)

    def norm_chunk(chunk, carry):
        columns = pl.ds(pl.multiple_of(chunk * norm_width, norm_width), norm_width)
        normed = normed_ref[:, columns] * inv_rms
        normed_ref[:, columns] = normed
        normed_b_ref[:, columns] = normed.astype(BF16)
        return carry

    lax.fori_loop(0, NORM_CHUNKS, norm_chunk, 0)

    pl.semaphore_wait(barrier, 2 + mp_count - 1)
    cot_copies = []
    for at, (slot, home) in enumerate(((rows, left), (rows + 1, right))):
        copy = pltpu.make_async_remote_copy(
            src_ref=cot_hbm.at[slot],
            dst_ref=cot_recv.at[at],
            send_sem=cot_send_sem.at[at],
            recv_sem=cot_recv_sem.at[at],
            device_id={"dp": home},
            device_id_type=MESH,
        )
        copy.start()
        cot_copies.append(copy)

    projected_ref[...] = jnp.zeros_like(projected_ref)

    def project(chunk, carry):
        for load in load_weights(chunk):
            load.wait()
        piece = pl.ds(pl.multiple_of(chunk * depth, depth), depth)
        part = normed_b_ref[:, piece]
        for which in range(3):
            projected_ref[which] += matmul(part, weights[which, piece, :])
        return carry

    lax.fori_loop(0, FORWARD_CHUNKS, project, 0)
    query_f32, key_f32, value_f32 = projected_ref[0], projected_ref[1], projected_ref[2]
    load_cot.wait()
    for copy in cot_copies:
        copy.wait()

    query = query_f32.astype(BF16)
    key = key_f32.astype(BF16)
    factor = 1.0 / math.sqrt(head)
    scores = jnp.where(key_ok, matmul(key, query, NT) * factor, -jnp.inf)
    exp_scores = jnp.exp(scores - jnp.max(scores, axis=0, keepdims=True))
    soft = exp_scores / jnp.sum(exp_scores, axis=0, keepdims=True)
    soft_b = soft.astype(BF16)
    value = value_f32.astype(BF16)
    projected = (query_f32, key_f32, value_f32)

    def moves(r, offset):
        return jnp.full((1, 1), move_ref[r], jnp.int32) == offset

    from_right = cot_recv[0].astype(F32)
    from_left = cot_recv[1].astype(F32)
    pieces = []
    for r in range(rows):
        moved = jnp.where(moves(r, 1), from_right, from_left)
        pieces.append(jnp.where(moves(r, 0), cot_ref[r].astype(F32), moved).astype(BF16))
    grad_out = matmul(permute, jnp.concatenate(pieces, axis=0))
    grad_out = jnp.where(query_ok, grad_out, 0.0).astype(BF16)

    grad_value = matmul(soft_b, grad_out).astype(BF16)
    grad_soft = matmul(value, grad_out, NT)
    row_inner = jnp.sum(soft * grad_soft, axis=0, keepdims=True)
    grad_scores = (soft * (grad_soft - row_inner) * factor).astype(BF16)
    grad_query = matmul(grad_scores, key, TN).astype(BF16)
    grad_key = matmul(grad_scores, query).astype(BF16)
    gradients = (grad_query, grad_key, grad_value)
    inner = jnp.zeros((total, 1), F32)
    for gradient, result in zip(gradients, projected):
        inner += jnp.sum(gradient.astype(F32) * result, axis=1, keepdims=True)
    inner = inner * (1.0 / width)

    back_width = width // BACK_CHUNKS
    half = back_width // 2

    def remote(source, target, send_sem, recv_sem, peer):
        return pltpu.make_async_remote_copy(
            src_ref=source,
            dst_ref=target,
            send_sem=send_sem,
            recv_sem=recv_sem,
            device_id={"mp": peer},
            device_id_type=MESH,
        )

    def direct(chunk, step):
        peer = lax.rem(my_mp + step, mp_count)
        return remote(
            part_send.at[chunk, peer],
            part_recv.at[chunk, step - 1],
            part_send_sem.at[chunk, step - 1],
            part_recv_sem.at[chunk, step - 1],
            peer,
        )

    def back(chunk, carry):
        piece = pl.ds(pl.multiple_of(chunk * back_width, back_width), back_width)
        head_grad = matmul(gradients[0], weights[0, piece, :], NT)
        head_grad += matmul(gradients[1], weights[1, piece, :], NT)
        head_grad += matmul(gradients[2], weights[2, piece, :], NT)
        head_part = (head_grad - normed_ref[:, piece] * inner) * inv_rms
        for s in range(mp_count):
            block = head_part[s * seg_total : (s + 1) * seg_total]
            stacked = jnp.concatenate([block[:, :half], block[:, half:]], axis=0)
            part_send[chunk, s] = stacked.astype(BF16)
        for step in range(1, mp_count):
            direct(chunk, step).start()
        return carry

    lax.fori_loop(0, BACK_CHUNKS, back, 0)

    context = jnp.where(query_ok, matmul(soft_b, value, TN), 0.0).astype(BF16)
    context = matmul(permute, context, TN)

    for at, offset in enumerate((1, -1)):
        leaving = jnp.zeros((length, head), F32)
        for r in range(rows):
            leaving = jnp.where(moves(r, offset), context[r * length : (r + 1) * length], leaving)
        ctx_send[at] = leaving.astype(BF16)
    ctx_copies = []
    for at, (slot, target) in enumerate(((rows, right), (rows + 1, left))):
        copy = pltpu.make_async_remote_copy(
            src_ref=ctx_send.at[at],
            dst_ref=context_ref.at[slot],
            send_sem=ctx_send_sem.at[at],
            recv_sem=ctx_recv_sem.at[at],
            device_id={"dp": target},
            device_id_type=MESH,
        )
        copy.start()
        ctx_copies.append(copy)
    for r in range(rows):
        own = jnp.where(moves(r, 0), context[r * length : (r + 1) * length], 0.0)
        context_ref[r] = own.astype(BF16)

    span_own = jnp.concatenate(
        [span_column(r, my_mp * seg, seg) for r in range(rows)], axis=0
    )
    def finish(chunk, carry):
        summed = part_send[chunk, my_mp].astype(F32)
        for step in range(1, mp_count):
            direct(chunk, step).wait_recv()
            summed += part_recv[chunk, step - 1].astype(F32)
        for part in range(2):
            block = jnp.where(
                span_own > 0.5, 0.0, summed[part * seg_total : (part + 1) * seg_total]
            ).astype(BF16)
            columns = pl.ds(pl.multiple_of(chunk * back_width + part * half, half), half)
            for r in range(rows):
                grad_ref[r, :, columns] = block[r * seg : (r + 1) * seg]
        for step in range(1, mp_count):
            direct(chunk, step).wait_send()
        return carry

    lax.fori_loop(0, BACK_CHUNKS, finish, 0)
    for copy in ctx_copies:
        copy.wait()


def store_kernel(context_ref, grad_ref, context_out, grad_out, sem):
    copies = [
        pltpu.make_async_copy(context_ref, context_out, sem.at[0]),
        pltpu.make_async_copy(grad_ref, grad_out, sem.at[1]),
    ]
    for copy in copies:
        copy.start()
    for copy in copies:
        copy.wait()


def store(context, grad):
    vmem = pl.BlockSpec(memory_space=pltpu.VMEM)
    hbm = pl.BlockSpec(memory_space=pltpu.HBM)
    return pl.pallas_call(
        store_kernel,
        out_shape=(pltpu.HBM(context.shape, BF16), pltpu.HBM(grad.shape, BF16)),
        in_specs=[vmem, vmem],
        out_specs=(hbm, hbm),
        scratch_shapes=[pltpu.SemaphoreType.DMA((2,))],
        compiler_params=pltpu.CompilerParams(vmem_limit_bytes=1024 * 1024),
    )(context, grad)


def shards(
    inputs,
    denoiser,
    span_mask,
    lengths,
    move_plan,
    mode_table,
    sentinel,
    w_query,
    w_key,
    w_value,
    cotangent,
):
    rows, length, width = inputs.shape
    head = w_query.shape[1]
    dp_count = lax.axis_size("dp")
    mp_count = lax.axis_size("mp")
    seg = length // mp_count
    total = rows * length
    block = (2 * rows * seg, width // BACK_CHUNKS // 2)
    vmem = pl.BlockSpec(memory_space=pltpu.VMEM)
    anywhere = pl.BlockSpec(memory_space=pltpu.HBM)
    dma = pltpu.SemaphoreType.DMA
    context, grad = pl.pallas_call(
        functools.partial(kernel, dp_count, mp_count),
        out_shape=(
            pltpu.VMEM(cotangent.shape, BF16),
            pltpu.VMEM((rows, seg, width), BF16),
        ),
        in_specs=[anywhere] * 11,
        out_specs=(vmem, vmem),
        scratch_shapes=[
            pltpu.SMEM((rows,), jnp.int32),
            pltpu.SMEM((rows,), jnp.int32),
            pltpu.SMEM((rows,), jnp.int32),
            pltpu.VMEM((rows, length), jnp.int32),
            pltpu.VMEM(mode_table.shape, BF16),
            pltpu.VMEM((width // LANES, LANES), BF16),
            pltpu.VMEM((rows, length, width), BF16),
            pltpu.VMEM((rows, length, head), BF16),
            pltpu.VMEM((3, width, head), BF16),
            pltpu.VMEM((1, width), F32),
            pltpu.VMEM((total, width), F32),
            pltpu.VMEM((total, width), BF16),
            pltpu.VMEM((3, total, head), F32),
            pltpu.VMEM((2, length, head), BF16),
            pltpu.VMEM((2, length, head), BF16),
            pltpu.VMEM((BACK_CHUNKS, mp_count) + block, BF16),
            pltpu.VMEM((BACK_CHUNKS, mp_count - 1) + block, BF16),
            dma((6,)),
            dma((2,)),
            dma((3, FORWARD_CHUNKS)),
            dma((2,)),
            dma((2,)),
            dma((2,)),
            dma((2,)),
            dma((BACK_CHUNKS, mp_count - 1)),
            dma((BACK_CHUNKS, mp_count - 1)),
        ],
        compiler_params=pltpu.CompilerParams(
            collective_id=0, has_side_effects=True, vmem_limit_bytes=48 * 1024 * 1024
        ),
        cost_estimate=pl.CostEstimate(
            flops=4 * total * width * 3 * head,
            bytes_accessed=2 * 3 * width * head + 4 * total * width,
            transcendentals=total * total,
        ),
    )(
        *[
            pltpu.with_memory_space_constraint(operand, pltpu.HBM)
            for operand in (
                denoiser,
                lengths,
                move_plan,
                span_mask,
                mode_table,
                sentinel.reshape(width // LANES, LANES),
                inputs,
                cotangent,
                w_query,
                w_key,
                w_value,
            )
        ]
    )
    return store(context, grad)


def solution(mesh):
    return jax.shard_map(
        shards,
        mesh=mesh,
        in_specs=(
            P("dp", None, None),
            P("dp"),
            P("dp", None),
            P("dp"),
            P("dp"),
            P(),
            P(),
            P(None, "mp"),
            P(None, "mp"),
            P(None, "mp"),
            P("dp", None, "mp"),
        ),
        out_specs=(P("dp", None, "mp"), P("dp", "mp", None)),
        check_vma=False,
    )
```

```python
import functools
import math

import jax
import jax.numpy as jnp
from jax import lax
from jax.experimental import pallas as pl
from jax.experimental.pallas import tpu as pltpu
from jax.sharding import PartitionSpec as P

MESH = pl.DeviceIdType.MESH
F32 = jnp.float32
BF16 = jnp.bfloat16
NT = (((1,), (1,)), ((), ()))
TN = (((0,), (0,)), ((), ()))
NN = (((1,), (0,)), ((), ()))

FORWARD_CHUNKS = 2
BACK_CHUNKS = 4
NORM_CHUNKS = 4
LANES = 128


def matmul(a, b, dims=NN):
    return lax.dot_general(a, b, dims, preferred_element_type=F32)


def kernel(
    dp_count,
    mp_count,
    denoiser_hbm,
    lengths_hbm,
    move_hbm,
    span_hbm,
    table_hbm,
    sentinel_hbm,
    inputs_hbm,
    cot_hbm,
    wq_hbm,
    wk_hbm,
    wv_hbm,
    context_ref,
    grad_ref,
    denoiser_ref,
    lengths_ref,
    move_ref,
    span_ref,
    table_ref,
    sentinel_ref,
    inputs_ref,
    cot_ref,
    weights,
    normed_ref,
    normed_b_ref,
    cot_recv,
    ctx_send,
    part_send,
    part_recv,
    small_sem,
    in_sem,
    w_sem,
    cot_send_sem,
    cot_recv_sem,
    ctx_send_sem,
    ctx_recv_sem,
    part_send_sem,
    part_recv_sem,
):
    rows, length, width = inputs_ref.shape
    head = weights.shape[2]
    seg = length // mp_count
    total = rows * length
    seg_total = rows * seg
    mode_count = table_ref.shape[0]
    my_dp = lax.axis_index("dp")
    my_mp = lax.axis_index("mp")
    right = lax.rem(my_dp + 1, dp_count)
    left = lax.rem(my_dp + dp_count - 1, dp_count)

    barrier = pltpu.get_barrier_semaphore()
    for neighbour in (left, right):
        pl.semaphore_signal(barrier, inc=1, device_id={"dp": neighbour}, device_id_type=MESH)
    for step in range(1, mp_count):
        pl.semaphore_signal(
            barrier,
            inc=1,
            device_id={"mp": lax.rem(my_mp + step, mp_count)},
            device_id_type=MESH,
        )

    small_loads = []
    for at, (source, target) in enumerate(
        (
            (denoiser_hbm, denoiser_ref),
            (lengths_hbm, lengths_ref),
            (move_hbm, move_ref),
            (span_hbm, span_ref),
            (table_hbm, table_ref),
            (sentinel_hbm, sentinel_ref),
        )
    ):
        load = pltpu.make_async_copy(source, target, small_sem.at[at])
        load.start()
        small_loads.append(load)
    load_inputs = pltpu.make_async_copy(inputs_hbm, inputs_ref, in_sem.at[0])
    load_inputs.start()
    load_cot = pltpu.make_async_copy(cot_hbm.at[pl.ds(0, rows)], cot_ref, in_sem.at[1])
    load_cot.start()
    depth = width // FORWARD_CHUNKS
    loads = []
    for which, source in enumerate((wq_hbm, wk_hbm, wv_hbm)):
        for chunk in range(FORWARD_CHUNKS):
            piece = pl.ds(chunk * depth, depth)
            load = pltpu.make_async_copy(
                source.at[piece], weights.at[which, piece], w_sem.at[which, chunk]
            )
            load.start()
            loads.append(load)

    for load in small_loads:
        load.wait()

    def split(index):
        row = lax.rem(lax.div(index, seg), rows)
        place = lax.div(index, seg_total) * seg + lax.rem(index, seg)
        return row, place

    def per_row(row, ref):
        value = jnp.zeros_like(row)
        for r in range(rows):
            value = jnp.where(row == r, ref[r], value)
        return value

    col_row, col_place = split(lax.broadcasted_iota(jnp.int32, (total, 1), 0))
    lane_row, _ = split(lax.broadcasted_iota(jnp.int32, (1, total), 1))
    natural_lane = lax.broadcasted_iota(jnp.int32, (total, total), 1)
    permute = (natural_lane == col_row * length + col_place).astype(F32).astype(BF16)
    col_len = per_row(col_row, lengths_ref)
    key_ok = (col_row == lane_row) & (col_place < jnp.maximum(col_len, 1))
    query_ok = col_place < col_len

    def span_column(r, start, count):
        flags = jnp.broadcast_to(span_ref[r : r + 1, :], (count, length))
        place = lax.broadcasted_iota(jnp.int32, (count, length), 0) + start
        lane = lax.broadcasted_iota(jnp.int32, (count, length), 1)
        return jnp.sum(
            jnp.where((place == lane) & (flags == 1), 1.0, 0.0), axis=1, keepdims=True
        )

    span_natural = [span_column(r, 0, length) for r in range(rows)]
    denoiser_col = [jnp.full((1, 1), denoiser_ref[r], jnp.int32) for r in range(rows)]

    load_inputs.wait()
    norm_width = width // NORM_CHUNKS
    squares = jnp.zeros((total, 1), F32)
    for chunk in range(NORM_CHUNKS):
        columns = pl.ds(chunk * norm_width, norm_width)
        lines = norm_width // LANES
        lines_f32 = sentinel_ref[pl.ds(chunk * lines, lines), :].astype(F32)
        sentinel = jnp.concatenate([lines_f32[i : i + 1] for i in range(lines)], axis=1)
        table = table_ref[:, columns].astype(F32)
        pieces = []
        for r in range(rows):
            mode_row = jnp.zeros((1, norm_width), F32)
            for mode in range(mode_count):
                mode_row = jnp.where(denoiser_col[r] == mode, table[mode : mode + 1], mode_row)
            plain = inputs_ref[r, :, columns].astype(F32) + mode_row
            pieces.append(jnp.where(span_natural[r] > 0.5, sentinel, plain).astype(BF16))
        shaped = matmul(permute, jnp.concatenate(pieces, axis=0))
        normed_ref[:, columns] = shaped
        squares += jnp.sum(shaped * shaped, axis=1, keepdims=True)
    inv_rms = lax.rsqrt(squares * (1.0 / width) + 1e-06)
    for chunk in range(NORM_CHUNKS):
        columns = pl.ds(chunk * norm_width, norm_width)
        normed = normed_ref[:, columns] * inv_rms
        normed_ref[:, columns] = normed
        normed_b_ref[:, columns] = normed.astype(BF16)

    pl.semaphore_wait(barrier, 2 + mp_count - 1)
    cot_copies = []
    for at, (slot, home) in enumerate(((rows, left), (rows + 1, right))):
        copy = pltpu.make_async_remote_copy(
            src_ref=cot_hbm.at[slot],
            dst_ref=cot_recv.at[at],
            send_sem=cot_send_sem.at[at],
            recv_sem=cot_recv_sem.at[at],
            device_id={"dp": home},
            device_id_type=MESH,
        )
        copy.start()
        cot_copies.append(copy)

    def project(which, chunk):
        piece = pl.ds(chunk * depth, depth)
        return matmul(normed_b_ref[:, piece], weights[which, piece, :])

    query_f32 = jnp.zeros((total, head), F32)
    key_f32 = jnp.zeros((total, head), F32)
    for chunk in range(FORWARD_CHUNKS):
        loads[chunk].wait()
        query_f32 += project(0, chunk)
    for chunk in range(FORWARD_CHUNKS):
        loads[FORWARD_CHUNKS + chunk].wait()
        key_f32 += project(1, chunk)
    for chunk in range(FORWARD_CHUNKS):
        loads[2 * FORWARD_CHUNKS + chunk].wait()
    load_cot.wait()
    for copy in cot_copies:
        copy.wait()

    query = query_f32.astype(BF16)
    key = key_f32.astype(BF16)
    factor = 1.0 / math.sqrt(head)
    scores = jnp.where(key_ok, matmul(key, query, NT) * factor, -jnp.inf)
    value_f32 = project(2, 0)
    for chunk in range(1, FORWARD_CHUNKS):
        value_f32 += project(2, chunk)
    exp_scores = jnp.exp(scores - jnp.max(scores, axis=0, keepdims=True))
    soft = exp_scores / jnp.sum(exp_scores, axis=0, keepdims=True)
    soft_b = soft.astype(BF16)
    value = value_f32.astype(BF16)
    projected = (query_f32, key_f32, value_f32)

    def moves(r, offset):
        return jnp.full((1, 1), move_ref[r], jnp.int32) == offset

    from_right = cot_recv[0].astype(F32)
    from_left = cot_recv[1].astype(F32)
    pieces = []
    for r in range(rows):
        moved = jnp.where(moves(r, 1), from_right, from_left)
        pieces.append(jnp.where(moves(r, 0), cot_ref[r].astype(F32), moved).astype(BF16))
    grad_out = matmul(permute, jnp.concatenate(pieces, axis=0))
    grad_out = jnp.where(query_ok, grad_out, 0.0).astype(BF16)

    grad_value = matmul(soft_b, grad_out).astype(BF16)
    grad_soft = matmul(value, grad_out, NT)
    row_inner = jnp.sum(soft * grad_soft, axis=0, keepdims=True)
    grad_scores = (soft * (grad_soft - row_inner) * factor).astype(BF16)
    grad_query = matmul(grad_scores, key, TN).astype(BF16)
    grad_key = matmul(grad_scores, query).astype(BF16)
    gradients = (grad_query, grad_key, grad_value)
    inner = jnp.zeros((total, 1), F32)
    for gradient, result in zip(gradients, projected):
        inner += jnp.sum(gradient.astype(F32) * result, axis=1, keepdims=True)
    inner = inner * (1.0 / width)

    back_width = width // BACK_CHUNKS
    half = back_width // 2

    def remote(source, target, send_sem, recv_sem, peer):
        return pltpu.make_async_remote_copy(
            src_ref=source,
            dst_ref=target,
            send_sem=send_sem,
            recv_sem=recv_sem,
            device_id={"mp": peer},
            device_id_type=MESH,
        )

    joined = jnp.concatenate(gradients, axis=1)

    def back(chunk):
        piece = pl.ds(chunk * back_width, back_width)
        beside = jnp.concatenate([weights[which, piece, :] for which in range(3)], axis=1)
        return matmul(beside, joined, NT).T

    def direct(chunk, step):
        peer = lax.rem(my_mp + step, mp_count)
        return remote(
            part_send.at[chunk, peer],
            part_recv.at[chunk, step - 1],
            part_send_sem.at[chunk, step - 1],
            part_recv_sem.at[chunk, step - 1],
            peer,
        )

    head_grad = back(0)
    for chunk in range(BACK_CHUNKS):
        piece = pl.ds(chunk * back_width, back_width)
        following = back(chunk + 1) if chunk + 1 < BACK_CHUNKS else None
        head_part = (head_grad - normed_ref[:, piece] * inner) * inv_rms
        for s in range(mp_count):
            block = head_part[s * seg_total : (s + 1) * seg_total]
            stacked = jnp.concatenate([block[:, :half], block[:, half:]], axis=0)
            part_send[chunk, s] = stacked.astype(BF16)
        for step in range(1, mp_count):
            direct(chunk, step).start()
        head_grad = following

    context = jnp.where(query_ok, matmul(soft_b, value, TN), 0.0).astype(BF16)
    context = matmul(permute, context, TN)

    for at, offset in enumerate((1, -1)):
        leaving = jnp.zeros((length, head), F32)
        for r in range(rows):
            leaving = jnp.where(moves(r, offset), context[r * length : (r + 1) * length], leaving)
        ctx_send[at] = leaving.astype(BF16)
    ctx_copies = []
    for at, (slot, target) in enumerate(((rows, right), (rows + 1, left))):
        copy = pltpu.make_async_remote_copy(
            src_ref=ctx_send.at[at],
            dst_ref=context_ref.at[slot],
            send_sem=ctx_send_sem.at[at],
            recv_sem=ctx_recv_sem.at[at],
            device_id={"dp": target},
            device_id_type=MESH,
        )
        copy.start()
        ctx_copies.append(copy)
    for r in range(rows):
        own = jnp.where(moves(r, 0), context[r * length : (r + 1) * length], 0.0)
        context_ref[r] = own.astype(BF16)

    span_own = jnp.concatenate(
        [span_column(r, my_mp * seg, seg) for r in range(rows)], axis=0
    )
    for chunk in range(BACK_CHUNKS):
        summed = part_send[chunk, my_mp].astype(F32)
        for step in range(1, mp_count):
            direct(chunk, step).wait_recv()
            summed += part_recv[chunk, step - 1].astype(F32)
        for part in range(2):
            block = jnp.where(
                span_own > 0.5, 0.0, summed[part * seg_total : (part + 1) * seg_total]
            ).astype(BF16)
            columns = pl.ds(chunk * back_width + part * half, half)
            for r in range(rows):
                grad_ref[r, :, columns] = block[r * seg : (r + 1) * seg]

    for chunk in range(BACK_CHUNKS):
        for step in range(1, mp_count):
            direct(chunk, step).wait_send()
    for copy in ctx_copies:
        copy.wait()


def store_kernel(context_ref, grad_ref, context_out, grad_out, sem):
    copies = [
        pltpu.make_async_copy(context_ref, context_out, sem.at[0]),
        pltpu.make_async_copy(grad_ref, grad_out, sem.at[1]),
    ]
    for copy in copies:
        copy.start()
    for copy in copies:
        copy.wait()


def store(context, grad):
    vmem = pl.BlockSpec(memory_space=pltpu.VMEM)
    hbm = pl.BlockSpec(memory_space=pltpu.HBM)
    return pl.pallas_call(
        store_kernel,
        out_shape=(pltpu.HBM(context.shape, BF16), pltpu.HBM(grad.shape, BF16)),
        in_specs=[vmem, vmem],
        out_specs=(hbm, hbm),
        scratch_shapes=[pltpu.SemaphoreType.DMA((2,))],
        compiler_params=pltpu.CompilerParams(vmem_limit_bytes=1024 * 1024),
    )(context, grad)


def shards(
    inputs,
    denoiser,
    span_mask,
    lengths,
    move_plan,
    mode_table,
    sentinel,
    w_query,
    w_key,
    w_value,
    cotangent,
):
    rows, length, width = inputs.shape
    head = w_query.shape[1]
    dp_count = lax.axis_size("dp")
    mp_count = lax.axis_size("mp")
    seg = length // mp_count
    total = rows * length
    block = (2 * rows * seg, width // BACK_CHUNKS // 2)
    vmem = pl.BlockSpec(memory_space=pltpu.VMEM)
    anywhere = pl.BlockSpec(memory_space=pltpu.HBM)
    dma = pltpu.SemaphoreType.DMA
    context, grad = pl.pallas_call(
        functools.partial(kernel, dp_count, mp_count),
        out_shape=(
            pltpu.VMEM(cotangent.shape, BF16),
            pltpu.VMEM((rows, seg, width), BF16),
        ),
        in_specs=[anywhere] * 11,
        out_specs=(vmem, vmem),
        scratch_shapes=[
            pltpu.SMEM((rows,), jnp.int32),
            pltpu.SMEM((rows,), jnp.int32),
            pltpu.SMEM((rows,), jnp.int32),
            pltpu.VMEM((rows, length), jnp.int32),
            pltpu.VMEM(mode_table.shape, BF16),
            pltpu.VMEM((width // LANES, LANES), BF16),
            pltpu.VMEM((rows, length, width), BF16),
            pltpu.VMEM((rows, length, head), BF16),
            pltpu.VMEM((3, width, head), BF16),
            pltpu.VMEM((total, width), F32),
            pltpu.VMEM((total, width), BF16),
            pltpu.VMEM((2, length, head), BF16),
            pltpu.VMEM((2, length, head), BF16),
            pltpu.VMEM((BACK_CHUNKS, mp_count) + block, BF16),
            pltpu.VMEM((BACK_CHUNKS, mp_count - 1) + block, BF16),
            dma((6,)),
            dma((2,)),
            dma((3, FORWARD_CHUNKS)),
            dma((2,)),
            dma((2,)),
            dma((2,)),
            dma((2,)),
            dma((BACK_CHUNKS, mp_count - 1)),
            dma((BACK_CHUNKS, mp_count - 1)),
        ],
        compiler_params=pltpu.CompilerParams(
            collective_id=0, has_side_effects=True, vmem_limit_bytes=48 * 1024 * 1024
        ),
        cost_estimate=pl.CostEstimate(
            flops=4 * total * width * 3 * head,
            bytes_accessed=2 * 3 * width * head + 4 * total * width,
            transcendentals=total * total,
        ),
    )(
        *[
            pltpu.with_memory_space_constraint(operand, pltpu.HBM)
            for operand in (
                denoiser,
                lengths,
                move_plan,
                span_mask,
                mode_table,
                sentinel.reshape(width // LANES, LANES),
                inputs,
                cotangent,
                w_query,
                w_key,
                w_value,
            )
        ]
    )
    return store(context, grad)


def solution(mesh):
    return jax.shard_map(
        shards,
        mesh=mesh,
        in_specs=(
            P("dp", None, None),
            P("dp"),
            P("dp", None),
            P("dp"),
            P("dp"),
            P(),
            P(),
            P(None, "mp"),
            P(None, "mp"),
            P(None, "mp"),
            P("dp", None, "mp"),
        ),
        out_specs=(P("dp", None, "mp"), P("dp", "mp", None)),
        check_vma=False,
    )
```

```python
import functools
import math

import jax
import jax.numpy as jnp
from jax import lax
from jax.experimental import pallas as pl
from jax.experimental.pallas import tpu as pltpu
from jax.sharding import PartitionSpec as P

MESH = pl.DeviceIdType.MESH
F32 = jnp.float32
BF16 = jnp.bfloat16
NT = (((1,), (1,)), ((), ()))
TN = (((0,), (0,)), ((), ()))
NN = (((1,), (0,)), ((), ()))

FORWARD_CHUNKS = 4
BACK_CHUNKS = 8
NORM_CHUNKS = 4
LANES = 128


def matmul(a, b, dims=NN):
    return lax.dot_general(a, b, dims, preferred_element_type=F32)


def kernel(
    dp_count,
    mp_count,
    denoiser_hbm,
    lengths_hbm,
    move_hbm,
    span_hbm,
    table_hbm,
    sentinel_hbm,
    inputs_hbm,
    cot_hbm,
    wq_hbm,
    wk_hbm,
    wv_hbm,
    context_ref,
    grad_ref,
    denoiser_ref,
    lengths_ref,
    move_ref,
    span_ref,
    table_ref,
    sentinel_ref,
    inputs_ref,
    cot_ref,
    weights,
    normed_ref,
    normed_b_ref,
    cot_recv,
    ctx_send,
    part_send,
    part_recv,
    pair_recv,
    pair_send,
    mate_recv,
    mate_sem,
    small_sem,
    in_sem,
    w_sem,
    cot_send_sem,
    cot_recv_sem,
    ctx_send_sem,
    ctx_recv_sem,
    part_send_sem,
    part_recv_sem,
):
    rows, length, width = inputs_ref.shape
    head = weights.shape[2]
    seg = length // mp_count
    total = rows * length
    seg_total = rows * seg
    mode_count = table_ref.shape[0]
    my_dp = lax.axis_index("dp")
    my_mp = lax.axis_index("mp")
    right = lax.rem(my_dp + 1, dp_count)
    left = lax.rem(my_dp + dp_count - 1, dp_count)

    barrier = pltpu.get_barrier_semaphore()
    for neighbour in (left, right):
        pl.semaphore_signal(barrier, inc=1, device_id={"dp": neighbour}, device_id_type=MESH)
    for step in range(1, mp_count):
        pl.semaphore_signal(
            barrier,
            inc=1,
            device_id={"mp": lax.rem(my_mp + step, mp_count)},
            device_id_type=MESH,
        )

    small_loads = []
    for at, (source, target) in enumerate(
        (
            (denoiser_hbm, denoiser_ref),
            (lengths_hbm, lengths_ref),
            (move_hbm, move_ref),
            (span_hbm, span_ref),
            (table_hbm, table_ref),
            (sentinel_hbm, sentinel_ref),
        )
    ):
        load = pltpu.make_async_copy(source, target, small_sem.at[at])
        load.start()
        small_loads.append(load)
    load_inputs = pltpu.make_async_copy(inputs_hbm, inputs_ref, in_sem.at[0])
    load_inputs.start()
    load_cot = pltpu.make_async_copy(cot_hbm.at[pl.ds(0, rows)], cot_ref, in_sem.at[1])
    load_cot.start()
    depth = width // FORWARD_CHUNKS
    loads = []
    for which, source in enumerate((wq_hbm, wk_hbm, wv_hbm)):
        for chunk in range(FORWARD_CHUNKS):
            piece = pl.ds(chunk * depth, depth)
            load = pltpu.make_async_copy(
                source.at[piece], weights.at[which, piece], w_sem.at[which, chunk]
            )
            load.start()
            loads.append(load)

    for load in small_loads:
        load.wait()

    def split(index):
        row = lax.rem(lax.div(index, seg), rows)
        place = lax.div(index, seg_total) * seg + lax.rem(index, seg)
        return row, place

    def per_row(row, ref):
        value = jnp.zeros_like(row)
        for r in range(rows):
            value = jnp.where(row == r, ref[r], value)
        return value

    col_row, col_place = split(lax.broadcasted_iota(jnp.int32, (total, 1), 0))
    lane_row, lane_place = split(lax.broadcasted_iota(jnp.int32, (1, total), 1))
    natural_lane = lax.broadcasted_iota(jnp.int32, (total, total), 1)
    permute = (natural_lane == col_row * length + col_place).astype(F32).astype(BF16)
    col_len = per_row(col_row, lengths_ref)
    key_ok = (col_row == lane_row) & (lane_place < jnp.maximum(col_len, 1))
    query_ok = col_place < col_len

    def span_column(r, start, count):
        flags = jnp.broadcast_to(span_ref[r : r + 1, :], (count, length))
        place = lax.broadcasted_iota(jnp.int32, (count, length), 0) + start
        lane = lax.broadcasted_iota(jnp.int32, (count, length), 1)
        return jnp.sum(
            jnp.where((place == lane) & (flags == 1), 1.0, 0.0), axis=1, keepdims=True
        )

    span_natural = [span_column(r, 0, length) for r in range(rows)]
    denoiser_col = [jnp.full((1, 1), denoiser_ref[r], jnp.int32) for r in range(rows)]

    load_inputs.wait()
    norm_width = width // NORM_CHUNKS
    squares = jnp.zeros((total, 1), F32)
    for chunk in range(NORM_CHUNKS):
        columns = pl.ds(chunk * norm_width, norm_width)
        lines = norm_width // LANES
        lines_f32 = sentinel_ref[pl.ds(chunk * lines, lines), :].astype(F32)
        sentinel = jnp.concatenate([lines_f32[i : i + 1] for i in range(lines)], axis=1)
        table = table_ref[:, columns].astype(F32)
        pieces = []
        for r in range(rows):
            mode_row = jnp.zeros((1, norm_width), F32)
            for mode in range(mode_count):
                mode_row = jnp.where(denoiser_col[r] == mode, table[mode : mode + 1], mode_row)
            plain = inputs_ref[r, :, columns].astype(F32) + mode_row
            pieces.append(jnp.where(span_natural[r] > 0.5, sentinel, plain).astype(BF16))
        shaped = matmul(permute, jnp.concatenate(pieces, axis=0))
        normed_ref[:, columns] = shaped
        squares += jnp.sum(shaped * shaped, axis=1, keepdims=True)
    inv_rms = lax.rsqrt(squares * (1.0 / width) + 1e-06)
    for chunk in range(NORM_CHUNKS):
        columns = pl.ds(chunk * norm_width, norm_width)
        normed = normed_ref[:, columns] * inv_rms
        normed_ref[:, columns] = normed
        normed_b_ref[:, columns] = normed.astype(BF16)

    pl.semaphore_wait(barrier, 2 + mp_count - 1)
    cot_copies = []
    for at, (slot, home) in enumerate(((rows, left), (rows + 1, right))):
        copy = pltpu.make_async_remote_copy(
            src_ref=cot_hbm.at[slot],
            dst_ref=cot_recv.at[at],
            send_sem=cot_send_sem.at[at],
            recv_sem=cot_recv_sem.at[at],
            device_id={"dp": home},
            device_id_type=MESH,
        )
        copy.start()
        cot_copies.append(copy)

    def project(which, chunk):
        piece = pl.ds(chunk * depth, depth)
        return matmul(normed_b_ref[:, piece], weights[which, piece, :])

    query_f32 = jnp.zeros((total, head), F32)
    key_f32 = jnp.zeros((total, head), F32)
    for chunk in range(FORWARD_CHUNKS):
        loads[chunk].wait()
        query_f32 += project(0, chunk)
    for chunk in range(FORWARD_CHUNKS):
        loads[FORWARD_CHUNKS + chunk].wait()
        key_f32 += project(1, chunk)
    for chunk in range(FORWARD_CHUNKS):
        loads[2 * FORWARD_CHUNKS + chunk].wait()
    load_cot.wait()
    for copy in cot_copies:
        copy.wait()

    query = query_f32.astype(BF16)
    key = key_f32.astype(BF16)
    factor = 1.0 / math.sqrt(head)
    scores = jnp.where(key_ok, matmul(query, key, NT) * factor, -jnp.inf)
    value_f32 = project(2, 0)
    for chunk in range(1, FORWARD_CHUNKS):
        value_f32 += project(2, chunk)
    exp_scores = jnp.exp(scores - jnp.max(scores, axis=1, keepdims=True))
    soft = exp_scores / jnp.sum(exp_scores, axis=1, keepdims=True)
    soft_b = soft.astype(BF16)
    value = value_f32.astype(BF16)
    projected = (query_f32, key_f32, value_f32)

    def moves(r, offset):
        return jnp.full((1, 1), move_ref[r], jnp.int32) == offset

    from_right = cot_recv[0].astype(F32)
    from_left = cot_recv[1].astype(F32)
    pieces = []
    for r in range(rows):
        moved = jnp.where(moves(r, 1), from_right, from_left)
        pieces.append(jnp.where(moves(r, 0), cot_ref[r].astype(F32), moved).astype(BF16))
    grad_out = matmul(permute, jnp.concatenate(pieces, axis=0))
    grad_out = jnp.where(query_ok, grad_out, 0.0).astype(BF16)

    grad_value = matmul(soft_b, grad_out, TN).astype(BF16)
    grad_soft = matmul(grad_out, value, NT)
    row_inner = jnp.sum(soft * grad_soft, axis=1, keepdims=True)
    grad_scores = (soft * (grad_soft - row_inner) * factor).astype(BF16)
    grad_query = matmul(grad_scores, key).astype(BF16)
    grad_key = matmul(grad_scores, query, TN).astype(BF16)
    gradients = (grad_query, grad_key, grad_value)
    inner = jnp.zeros((total, 1), F32)
    for gradient, result in zip(gradients, projected):
        inner += jnp.sum(gradient.astype(F32) * result, axis=1, keepdims=True)
    inner = inner * (1.0 / width)

    back_width = width // BACK_CHUNKS
    half = back_width // 2
    paired = mp_count == 4
    mate = my_mp + 1 - 2 * lax.rem(my_mp, 2)
    other = 2 - 2 * lax.div(my_mp, 2)
    outer = (my_mp == 0) | (my_mp == mp_count - 1)

    def remote(source, target, send_sem, recv_sem, peer):
        return pltpu.make_async_remote_copy(
            src_ref=source,
            dst_ref=target,
            send_sem=send_sem,
            recv_sem=recv_sem,
            device_id={"mp": peer},
            device_id_type=MESH,
        )

    def back(chunk):
        piece = pl.ds(chunk * back_width, back_width)
        head_grad = matmul(gradients[0], weights[0, piece, :], NT)
        head_grad += matmul(gradients[1], weights[1, piece, :], NT)
        head_grad += matmul(gradients[2], weights[2, piece, :], NT)
        return head_grad

    def to_mate(chunk):
        return remote(
            part_send.at[chunk, pl.ds(other, 2)],
            pair_recv.at[chunk],
            part_send_sem.at[chunk, 0],
            part_recv_sem.at[chunk, 0],
            mate,
        )

    def from_inner(chunk, j):
        return remote(
            pair_send.at[chunk, j],
            part_recv.at[chunk, 0],
            part_send_sem.at[chunk, 1 + j],
            part_recv_sem.at[chunk, 1],
            other + j,
        )

    def direct(chunk, step):
        peer = lax.rem(my_mp + step, mp_count)
        return remote(
            part_send.at[chunk, peer],
            part_recv.at[chunk, step - 1],
            part_send_sem.at[chunk, step - 1],
            part_recv_sem.at[chunk, step - 1],
            peer,
        )

    head_grad = back(0)
    for chunk in range(BACK_CHUNKS):
        piece = pl.ds(chunk * back_width, back_width)
        following = back(chunk + 1) if chunk + 1 < BACK_CHUNKS else None
        head_part = (head_grad - normed_ref[:, piece] * inner) * inv_rms
        for s in range(mp_count):
            block = head_part[s * seg_total : (s + 1) * seg_total]
            stacked = jnp.concatenate([block[:, :half], block[:, half:]], axis=0)
            part_send[chunk, s] = stacked.astype(BF16)
        if paired:

            @pl.when(outer)
            def _():
                to_mate(chunk).start()

        else:
            for step in range(1, mp_count):
                direct(chunk, step).start()
        head_grad = following

    context = jnp.where(query_ok, matmul(soft_b, value), 0.0).astype(BF16)
    context = matmul(permute, context, TN)

    for at, offset in enumerate((1, -1)):
        leaving = jnp.zeros((length, head), F32)
        for r in range(rows):
            leaving = jnp.where(moves(r, offset), context[r * length : (r + 1) * length], leaving)
        ctx_send[at] = leaving.astype(BF16)
    ctx_copies = []
    for at, (slot, target) in enumerate(((rows, right), (rows + 1, left))):
        copy = pltpu.make_async_remote_copy(
            src_ref=ctx_send.at[at],
            dst_ref=context_ref.at[slot],
            send_sem=ctx_send_sem.at[at],
            recv_sem=ctx_recv_sem.at[at],
            device_id={"dp": target},
            device_id_type=MESH,
        )
        copy.start()
        ctx_copies.append(copy)
    for r in range(rows):
        own = jnp.where(moves(r, 0), context[r * length : (r + 1) * length], 0.0)
        context_ref[r] = own.astype(BF16)

    def own_pair(chunk):
        return remote(
            part_send.at[chunk, mate],
            mate_recv.at[chunk],
            mate_sem.at[0, chunk],
            mate_sem.at[1, chunk],
            mate,
        )

    if paired:

        @pl.when(outer)
        def _():
            for chunk in range(BACK_CHUNKS):
                to_mate(chunk).wait_send()

        for chunk in range(BACK_CHUNKS):
            own_pair(chunk).start()

        @pl.when(jnp.logical_not(outer))
        def _():
            for chunk in range(BACK_CHUNKS):
                to_mate(chunk).wait_recv()
                for j in range(2):
                    partial = part_send[chunk, other + j].astype(F32)
                    partial += pair_recv[chunk, j].astype(F32)
                    pair_send[chunk, j] = partial.astype(BF16)
                    from_inner(chunk, j).start()


    span_own = jnp.concatenate(
        [span_column(r, my_mp * seg, seg) for r in range(rows)], axis=0
    )
    for chunk in range(BACK_CHUNKS):
        summed = part_send[chunk, my_mp].astype(F32)
        if paired:
            own_pair(chunk).wait_recv()
            summed += mate_recv[chunk].astype(F32)
            from_inner(chunk, 0).wait_recv()
            summed += part_recv[chunk, 0].astype(F32)
        else:
            for step in range(1, mp_count):
                direct(chunk, step).wait_recv()
                summed += part_recv[chunk, step - 1].astype(F32)
        for part in range(2):
            block = jnp.where(
                span_own > 0.5, 0.0, summed[part * seg_total : (part + 1) * seg_total]
            ).astype(BF16)
            columns = pl.ds(chunk * back_width + part * half, half)
            for r in range(rows):
                grad_ref[r, :, columns] = block[r * seg : (r + 1) * seg]

    if paired:
        for chunk in range(BACK_CHUNKS):
            own_pair(chunk).wait_send()

        @pl.when(jnp.logical_not(outer))
        def _():
            for chunk in range(BACK_CHUNKS):
                for j in range(2):
                    from_inner(chunk, j).wait_send()

    else:
        for chunk in range(BACK_CHUNKS):
            for step in range(1, mp_count):
                direct(chunk, step).wait_send()
    for copy in ctx_copies:
        copy.wait()


def store_kernel(context_ref, grad_ref, context_out, grad_out, sem):
    copies = [
        pltpu.make_async_copy(context_ref, context_out, sem.at[0]),
        pltpu.make_async_copy(grad_ref, grad_out, sem.at[1]),
    ]
    for copy in copies:
        copy.start()
    for copy in copies:
        copy.wait()


def store(context, grad):
    vmem = pl.BlockSpec(memory_space=pltpu.VMEM)
    hbm = pl.BlockSpec(memory_space=pltpu.HBM)
    return pl.pallas_call(
        store_kernel,
        out_shape=(pltpu.HBM(context.shape, BF16), pltpu.HBM(grad.shape, BF16)),
        in_specs=[vmem, vmem],
        out_specs=(hbm, hbm),
        scratch_shapes=[pltpu.SemaphoreType.DMA((2,))],
        compiler_params=pltpu.CompilerParams(vmem_limit_bytes=1024 * 1024),
    )(context, grad)


def shards(
    inputs,
    denoiser,
    span_mask,
    lengths,
    move_plan,
    mode_table,
    sentinel,
    w_query,
    w_key,
    w_value,
    cotangent,
):
    rows, length, width = inputs.shape
    head = w_query.shape[1]
    dp_count = lax.axis_size("dp")
    mp_count = lax.axis_size("mp")
    seg = length // mp_count
    total = rows * length
    block = (2 * rows * seg, width // BACK_CHUNKS // 2)
    vmem = pl.BlockSpec(memory_space=pltpu.VMEM)
    anywhere = pl.BlockSpec(memory_space=pltpu.HBM)
    dma = pltpu.SemaphoreType.DMA
    context, grad = pl.pallas_call(
        functools.partial(kernel, dp_count, mp_count),
        out_shape=(
            pltpu.VMEM(cotangent.shape, BF16),
            pltpu.VMEM((rows, seg, width), BF16),
        ),
        in_specs=[anywhere] * 11,
        out_specs=(vmem, vmem),
        scratch_shapes=[
            pltpu.SMEM((rows,), jnp.int32),
            pltpu.SMEM((rows,), jnp.int32),
            pltpu.SMEM((rows,), jnp.int32),
            pltpu.VMEM((rows, length), jnp.int32),
            pltpu.VMEM(mode_table.shape, BF16),
            pltpu.VMEM((width // LANES, LANES), BF16),
            pltpu.VMEM((rows, length, width), BF16),
            pltpu.VMEM((rows, length, head), BF16),
            pltpu.VMEM((3, width, head), BF16),
            pltpu.VMEM((total, width), F32),
            pltpu.VMEM((total, width), BF16),
            pltpu.VMEM((2, length, head), BF16),
            pltpu.VMEM((2, length, head), BF16),
            pltpu.VMEM((BACK_CHUNKS, mp_count) + block, BF16),
            pltpu.VMEM((BACK_CHUNKS, mp_count - 1) + block, BF16),
            pltpu.VMEM((BACK_CHUNKS, 2) + block, BF16),
            pltpu.VMEM((BACK_CHUNKS, 2) + block, BF16),
            pltpu.VMEM((BACK_CHUNKS,) + block, BF16),
            dma((2, BACK_CHUNKS)),
            dma((6,)),
            dma((2,)),
            dma((3, FORWARD_CHUNKS)),
            dma((2,)),
            dma((2,)),
            dma((2,)),
            dma((2,)),
            dma((BACK_CHUNKS, mp_count - 1)),
            dma((BACK_CHUNKS, mp_count - 1)),
        ],
        compiler_params=pltpu.CompilerParams(
            collective_id=0, has_side_effects=True, vmem_limit_bytes=48 * 1024 * 1024
        ),
        cost_estimate=pl.CostEstimate(
            flops=4 * total * width * 3 * head,
            bytes_accessed=2 * 3 * width * head + 4 * total * width,
            transcendentals=total * total,
        ),
    )(
        *[
            pltpu.with_memory_space_constraint(operand, pltpu.HBM)
            for operand in (
                denoiser,
                lengths,
                move_plan,
                span_mask,
                mode_table,
                sentinel.reshape(width // LANES, LANES),
                inputs,
                cotangent,
                w_query,
                w_key,
                w_value,
            )
        ]
    )
    return store(context, grad)


def solution(mesh):
    return jax.shard_map(
        shards,
        mesh=mesh,
        in_specs=(
            P("dp", None, None),
            P("dp"),
            P("dp", None),
            P("dp"),
            P("dp"),
            P(),
            P(),
            P(None, "mp"),
            P(None, "mp"),
            P(None, "mp"),
            P("dp", None, "mp"),
        ),
        out_specs=(P("dp", None, "mp"), P("dp", "mp", None)),
        check_vma=False,
    )
```
